32 devices in a mesh: dp: 4 (over y, x), ctx: 8 (over z, core).
Axes of the slice: x: 2, y: 2, z: 4, core: 2. Of those that a mesh axis runs over, the one named last changes fastest.
Arguments:
- queries: bfloat16 [8, 512, 2560], P('ctx', 'dp'), may hold values from -20 to 20
- key_states: bfloat16 [8, 512, 2560], P('ctx', 'dp'), may hold values from -20 to 20
- values: bfloat16 [8, 512, 2560], P('ctx', 'dp'), may hold values from -6 to 6
- out_grad: bfloat16 [8, 512, 2560], P('ctx', 'dp'), may hold values from -6 to 6
- block_links: int32 [2, 4], P(None, 'dp'), may hold values from -1 to 2, as said below
- sink_logit: float32 [20], replicated, may hold values from 4 to 8
Outputs:
- query_grad: bfloat16 [8, 512, 2560], P('ctx', 'dp')
- key_grad: bfloat16 [8, 512, 2560], P('ctx', 'dp')
- value_grad: bfloat16 [8, 512, 2560], P('ctx', 'dp')
- sink_grad: float32 [20], replicated
The draws below stay inside these ranges and needn't reach their ends.
Inputs may be any that keep to these rules, and one draw needn't show every extreme that they name: block_links[j, b] is either -1 or b - 2**j; it is -1 wherever b - 2**j < 0; block_links[0, 3] is 2.
All inputs are finite; a program needn't handle non-finite values.
Results may differ from the reference program's by a relative error of at most 0.023.
Values may be sent and summed in bfloat16 or wider, within the bound.
No kernel may reach another device: no remote copies, remote signals or barrier semaphores. Data moves between devices by JAX's collectives and lax.ppermute only.
A program may use at most 64 MiB of HBM per device.

```python
import jax
import jax.numpy as jnp
from jax import lax

H = 20
HEAD = 128
BLOCK = 128
LEVELS = 2
BATCH = 8
SEQ = 512
NBLK = 4
BLK_DEV = 1


def draw_queries(key, part):
    own = jnp.clip(jax.random.normal(jax.random.fold_in(key, 31), (BATCH, SEQ, H * HEAD), jnp.float32), -4.0, 4.0)
    return own.astype(jnp.bfloat16)


def draw_key_states(key, part):
    own = jnp.clip(jax.random.normal(jax.random.fold_in(key, 32), (BATCH, SEQ, H * HEAD), jnp.float32), -4.0, 4.0)
    return own.astype(jnp.bfloat16)


def draw_block_links(key, part):
    block_ids = jnp.arange(NBLK, dtype=jnp.int32)[None, :]
    level_ids = jnp.arange(LEVELS, dtype=jnp.int32)[:, None]
    reach = (2 ** jnp.arange(LEVELS, dtype=jnp.int32))[:, None] * BLK_DEV
    target = block_ids - reach
    active = jax.random.randint(key, (LEVELS, NBLK), 0, 4) > 0
    forced = (level_ids == 0) & (block_ids == NBLK - 1)
    active = active | forced
    return jnp.where(active & (target >= 0), target, -1).astype(jnp.int32)


def shard_levels(rng, shape, split, smallest, high):
    level = 1.0
    for position, shards_of in split:
        steps = jax.random.uniform(jax.random.fold_in(jax.random.fold_in(rng, 6), position), (shards_of,), jnp.float32, smallest / len(split), high / len(split))
        level = level * jnp.repeat(jnp.exp(steps), shape[position] // shards_of).reshape((-1,) + (1,) * (len(shape) - 1 - position))
    return level


def noise(own_key, extent, scale, most, cuts=(), kind=jnp.bfloat16):
    values = jax.random.normal(own_key, extent, jnp.float32) * scale
    if len(cuts) > 0:
        values = shard_levels(own_key, extent, cuts, -0.22, 0.18) * values
    return jnp.clip(values, min=-most, max=most).astype(kind)


def setup_inputs(seed: int = 0) -> dict:
    arg_keys = jax.random.split(jax.random.key(seed), 7)
    queries = draw_queries(jax.random.fold_in(arg_keys[6], 71), 0)
    key_states = draw_key_states(jax.random.fold_in(arg_keys[6], 71), 0)
    values = noise(arg_keys[2], (BATCH, SEQ, H * HEAD), 1.0, 6.0, ((0, 8), (1, 4)))
    out_grad = noise(arg_keys[3], (BATCH, SEQ, H * HEAD), 1.0, 6.0, ((0, 8), (1, 4)))
    block_links = draw_block_links(jax.random.fold_in(arg_keys[6], 71), 0)
    sink_logit = jnp.clip(jax.random.uniform(arg_keys[5], (H,), jnp.float32, 4.0, 8.0), 4.0, 8.0)
    return {"queries": queries, "key_states": key_states, "values": values, "out_grad": out_grad, "block_links": block_links, "sink_logit": sink_logit}


NEG_FILL = -1.0e30


def causal_table(block_len):
    rows_iota = lax.broadcasted_iota(jnp.int32, (block_len, block_len), 0)
    cols_iota = lax.broadcasted_iota(jnp.int32, (block_len, block_len), 1)
    return rows_iota >= cols_iota


def reference(queries, key_states, values, out_grad, block_links, sink_logit):
    score_scale = HEAD ** -0.5
    valid_link = block_links >= 0
    safe_link = jnp.maximum(block_links, 0).astype(jnp.int32)
    causal = jnp.broadcast_to(causal_table(BLOCK), (NBLK, BLOCK, BLOCK))
    remote_masks = [jnp.broadcast_to(valid_link[level_num][:, None, None], (NBLK, BLOCK, BLOCK)) for level_num in range(LEVELS)]
    allowed = jnp.concatenate([causal] + remote_masks, axis=2)

    def one_sequence(item):
        q_seq, k_seq, v_seq, g_seq = item
        q_blocks = q_seq.reshape(NBLK, BLOCK, H, HEAD).astype(jnp.float32)
        k_blocks = k_seq.reshape(NBLK, BLOCK, H, HEAD).astype(jnp.float32)
        v_blocks = v_seq.reshape(NBLK, BLOCK, H, HEAD).astype(jnp.float32)
        g_blocks = g_seq.reshape(NBLK, BLOCK, H, HEAD).astype(jnp.float32)
        key_all = jnp.concatenate([k_blocks] + [k_blocks[safe_link[level_num]] for level_num in range(LEVELS)], axis=1)
        val_all = jnp.concatenate([v_blocks] + [v_blocks[safe_link[level_num]] for level_num in range(LEVELS)], axis=1)
        scores = jnp.einsum("bqhd,bkhd->bhqk", q_blocks, key_all) * score_scale
        scores = jnp.where(allowed[:, None], scores, NEG_FILL)
        row_max = jnp.maximum(jnp.max(scores, axis=-1), sink_logit[None, :, None])
        exp_scores = jnp.exp(scores - row_max[..., None])
        sink_exp = jnp.exp(sink_logit[None, :, None] - row_max)
        denominator = jnp.sum(exp_scores, axis=-1) + sink_exp
        soft_prob = exp_scores / denominator[..., None]
        sink_prob = sink_exp / denominator
        weights = lax.optimization_barrier(soft_prob.astype(jnp.bfloat16)).astype(jnp.float32)
        output = jnp.einsum("bhqk,bkhd->bqhd", weights, val_all).astype(jnp.bfloat16)
        output_wide = lax.optimization_barrier(output).astype(jnp.float32)
        row_delta = jnp.transpose(jnp.sum(g_blocks * output_wide, axis=-1), (0, 2, 1))
        prob_grad = jnp.einsum("bqhd,bkhd->bhqk", g_blocks, val_all)
        score_grad = (soft_prob * (prob_grad - row_delta[..., None])).astype(jnp.bfloat16)
        score_grad = lax.optimization_barrier(score_grad).astype(jnp.float32)
        query_grad = (jnp.einsum("bhqk,bkhd->bqhd", score_grad, key_all) * score_scale).astype(jnp.bfloat16)
        key_terms = jnp.einsum("bhqk,bqhd->bkhd", score_grad, q_blocks) * score_scale
        value_terms = jnp.einsum("bhqk,bqhd->bkhd", weights, g_blocks)
        key_grad = key_terms[:, :BLOCK]
        value_grad = value_terms[:, :BLOCK]
        for level_num in range(LEVELS):
            first_col = BLOCK * (1 + level_num)
            key_part = lax.optimization_barrier(key_terms[:, first_col:first_col + BLOCK].astype(jnp.bfloat16)).astype(jnp.float32)
            value_part = lax.optimization_barrier(value_terms[:, first_col:first_col + BLOCK].astype(jnp.bfloat16)).astype(jnp.float32)
            key_grad = key_grad.at[safe_link[level_num]].add(key_part)
            value_grad = value_grad.at[safe_link[level_num]].add(value_part)
        sink_term = -jnp.sum(sink_prob * row_delta, axis=(0, 2))
        return (query_grad.reshape(SEQ, H * HEAD),
                key_grad.astype(jnp.bfloat16).reshape(SEQ, H * HEAD),
                value_grad.astype(jnp.bfloat16).reshape(SEQ, H * HEAD),
                sink_term)

    grads = lax.map(one_sequence, (queries, key_states, values, out_grad))
    return (grads[0], grads[1], grads[2], jnp.sum(grads[3], axis=0))
```

```python
import functools

import jax
import jax.numpy as jnp
from jax import lax
from jax.experimental import pallas as pl
from jax.experimental.pallas import tpu as pltpu
from jax.sharding import PartitionSpec as P

BLOCK = 128
LEVELS = 2
FLAG_ROWS = 16
NEG_FILL = -1e30
ORDER = (3, 1, 2)


def pack_kernel(offset, width, share, links, *refs):
    arrays, outs, flags, sems, flag_sems = refs[:4], refs[4:8], refs[8], refs[9], refs[10]
    me = lax.axis_index("dp")
    live = [jnp.where(links[level, 0] >= 0, 1.0, 0.0) for level in range(LEVELS)]
    row = lax.broadcasted_iota(jnp.int32, (FLAG_ROWS, width), 0)
    flags[...] = jnp.where(row < 8, live[0], live[1]).astype(jnp.bfloat16)
    copies = []
    for mask in ORDER + (0,):
        start = pl.multiple_of((me ^ mask) * share + offset, BLOCK)
        for num, array in enumerate(arrays):
            copies.append(
                pltpu.make_async_copy(
                    array.at[0, :, pl.ds(start, width)],
                    outs[mask].at[pl.ds(num * BLOCK, BLOCK), :],
                    sems.at[mask, num],
                )
            )
        copies.append(
            pltpu.make_async_copy(
                flags, outs[mask].at[pl.ds(4 * BLOCK, FLAG_ROWS), :], flag_sems.at[mask]
            )
        )
    for copy in copies:
        copy.start()
    for copy in copies:
        copy.wait()


def pack(links, arrays, offset, width, share):
    rows = 4 * BLOCK + FLAG_ROWS
    return pl.pallas_call(
        functools.partial(pack_kernel, offset, width, share),
        out_shape=[jax.ShapeDtypeStruct((rows, width), jnp.bfloat16)] * 4,
        in_specs=[pl.BlockSpec(memory_space=pltpu.SMEM)] + [pl.BlockSpec(memory_space=pl.ANY)] * 4,
        out_specs=[pl.BlockSpec(memory_space=pl.ANY)] * 4,
        scratch_shapes=[
            pltpu.VMEM((FLAG_ROWS, width), jnp.bfloat16),
            pltpu.SemaphoreType.DMA((4, 4)),
            pltpu.SemaphoreType.DMA((4,)),
        ],
        cost_estimate=pl.CostEstimate(flops=0, bytes_accessed=16 * rows * width, transcendentals=0),
        name="pack",
    )(links, *arrays)


def dot_nt(a, b):
    return lax.dot_general(a, b, (((1,), (1,)), ((), ())), preferred_element_type=jnp.float32)


def dot_nn(a, b):
    return lax.dot_general(a, b, (((1,), (0,)), ((), ())), preferred_element_type=jnp.float32)


def dot_tn(a, b):
    return lax.dot_general(a, b, (((0,), (0,)), ((), ())), preferred_element_type=jnp.float32)


def attend_kernel(first_head, heads, heads_dev, score_scale, sink, *refs):
    ins, outs, sink_out = refs[:4], refs[4:8], refs[8]
    held, grads, in_sems, out_sems = refs[9:]
    me = lax.axis_index("dp")
    blocks = 4

    def columns(head):
        return pl.ds(head * BLOCK, BLOCK)

    loads = [
        [
            pltpu.make_async_copy(
                ins[mask].at[:, columns(head)],
                held.at[me ^ mask, :, columns(head)],
                in_sems.at[head, mask],
            )
            for mask in range(blocks)
        ]
        for head in range(heads)
    ]
    for group in loads:
        for copy in group:
            copy.start()
    keys_iota = lax.broadcasted_iota(jnp.int32, (BLOCK, BLOCK), 0)
    queries_iota = lax.broadcasted_iota(jnp.int32, (BLOCK, BLOCK), 1)
    causal = keys_iota <= queries_iota
    sink_out[...] = jnp.zeros_like(sink_out)
    stores = []
    for head in range(heads):
        for copy in loads[head]:
            copy.wait()
        cols = columns(head)

        def part(kind, first, last):
            return held[first : last + 1, kind * BLOCK : (kind + 1) * BLOCK, cols].reshape(
                (last + 1 - first) * BLOCK, BLOCK
            )

        sink_logit = sink[me * heads_dev + first_head + head]
        weight_blocks, grad_blocks = {}, {}
        sink_total = jnp.zeros((1, BLOCK), jnp.float32)
        for block in range(blocks):
            first = max(0, block - LEVELS)
            flags = held[block, 4 * BLOCK :, cols].astype(jnp.float32)
            scores = dot_nt(part(1, first, block), part(0, block, block)) * score_scale
            pieces = []
            for source in range(first, block + 1):
                piece = scores[(source - first) * BLOCK : (source - first + 1) * BLOCK]
                if source == block:
                    piece = jnp.where(causal, piece, NEG_FILL)
                else:
                    row = 8 * (block - source - 1)
                    piece = jnp.where(flags[row : row + 1] > 0.5, piece, NEG_FILL)
                pieces.append(piece)
            scores = jnp.concatenate(pieces, axis=0)
            row_max = jnp.maximum(jnp.max(scores, axis=0, keepdims=True), sink_logit)
            exp_scores = jnp.exp(scores - row_max)
            sink_exp = jnp.exp(sink_logit - row_max)
            scale = 1.0 / (jnp.sum(exp_scores, axis=0, keepdims=True) + sink_exp)
            soft_prob = exp_scores * scale
            prob_grad = dot_nt(part(2, first, block), part(3, block, block))
            row_delta = jnp.sum(soft_prob * prob_grad, axis=0, keepdims=True)
            sink_total = sink_total + sink_exp * scale * row_delta
            weights = soft_prob.astype(jnp.bfloat16)
            score_grad = (soft_prob * (prob_grad - row_delta)).astype(jnp.bfloat16)
            query_grad = dot_tn(score_grad, part(1, first, block)) * score_scale
            grads[block, 0:BLOCK, cols] = query_grad.astype(jnp.bfloat16)
            for source in range(first, block + 1):
                rows = slice((source - first) * BLOCK, (source - first + 1) * BLOCK)
                weight_blocks[block, source] = weights[rows]
                grad_blocks[block, source] = score_grad[rows]
        sink_out[head : head + 1, :] = sink_total
        for source in range(blocks):
            last = min(blocks - 1, source + LEVELS)
            score_grad = jnp.concatenate([grad_blocks[b, source] for b in range(source, last + 1)], axis=1)
            weights = jnp.concatenate([weight_blocks[b, source] for b in range(source, last + 1)], axis=1)
            key_grad = dot_nn(score_grad, part(0, source, last)) * score_scale
            value_grad = dot_nn(weights, part(3, source, last))
            grads[source, BLOCK : 2 * BLOCK, cols] = key_grad.astype(jnp.bfloat16)
            grads[source, 2 * BLOCK : 3 * BLOCK, cols] = value_grad.astype(jnp.bfloat16)
        for mask in ORDER + (0,):
            copy = pltpu.make_async_copy(
                grads.at[me ^ mask, :, cols], outs[mask].at[:, cols], out_sems.at[head, mask]
            )
            copy.start()
            stores.append(copy)
    for copy in stores:
        copy.wait()


def attend(sink_logit, packed, first_head, heads, heads_dev, score_scale):
    rows, width = packed[0].shape
    grad_rows = 3 * BLOCK
    return pl.pallas_call(
        functools.partial(attend_kernel, first_head, heads, heads_dev, score_scale),
        out_shape=[jax.ShapeDtypeStruct((grad_rows, width), jnp.bfloat16)] * 4
        + [jax.ShapeDtypeStruct((8, BLOCK), jnp.float32)],
        in_specs=[pl.BlockSpec(memory_space=pltpu.SMEM)] + [pl.BlockSpec(memory_space=pl.ANY)] * 4,
        out_specs=[pl.BlockSpec(memory_space=pl.ANY)] * 4 + [pl.BlockSpec(memory_space=pltpu.VMEM)],
        scratch_shapes=[
            pltpu.VMEM((4, rows, width), jnp.bfloat16),
            pltpu.VMEM((4, grad_rows, width), jnp.bfloat16),
            pltpu.SemaphoreType.DMA((heads, 4)),
            pltpu.SemaphoreType.DMA((heads, 4)),
        ],
        compiler_params=pltpu.CompilerParams(vmem_limit_bytes=32 * 2**20),
        cost_estimate=pl.CostEstimate(
            flops=heads * 9 * 5 * 2 * BLOCK**3,
            bytes_accessed=8 * (rows + grad_rows) * width,
            transcendentals=heads * 9 * BLOCK**2,
        ),
        name="attend",
    )(sink_logit, *packed)


def unpack_kernel(offset, width, share, *refs):
    ins, outs, sems = refs[:4], refs[-4:-1], refs[-1]
    me = lax.axis_index("dp")
    copies = []
    for mask in range(4):
        start = pl.multiple_of((me ^ mask) * share + offset, BLOCK)
        for num, out in enumerate(outs):
            copies.append(
                pltpu.make_async_copy(
                    ins[mask].at[pl.ds(num * BLOCK, BLOCK), :],
                    out.at[0, :, pl.ds(start, width)],
                    sems.at[mask, num],
                )
            )
    for copy in copies:
        copy.start()
    for copy in copies:
        copy.wait()


def unpack(parts, previous, offset, share, shape):
    width = parts[0].shape[1]
    return pl.pallas_call(
        functools.partial(unpack_kernel, offset, width, share),
        out_shape=[jax.ShapeDtypeStruct(shape, jnp.bfloat16)] * 3,
        in_specs=[pl.BlockSpec(memory_space=pl.ANY)] * (4 + len(previous)),
        out_specs=[pl.BlockSpec(memory_space=pl.ANY)] * 3,
        scratch_shapes=[pltpu.SemaphoreType.DMA((4, 3))],
        input_output_aliases={4 + num: num for num in range(len(previous))},
        cost_estimate=pl.CostEstimate(flops=0, bytes_accessed=8 * 3 * BLOCK * width, transcendentals=0),
        name="unpack",
    )(*parts, *previous)


def swap(value, axis, mask):
    return lax.ppermute(value, axis, [(i, i ^ mask) for i in range(lax.axis_size(axis))])


def head_shares_body(chunks, queries, key_states, values, out_grad, block_links, sink_logit):
    heads = sink_logit.shape[0]
    head_size = queries.shape[2] // heads
    score_scale = head_size ** (-0.5)
    heads_dev = heads // 4
    share = heads_dev * head_size
    arrays = (queries, key_states, values, out_grad)
    received, first = [], 0
    for count in chunks:
        packed = pack(block_links, arrays, first * head_size, count * head_size, share)
        moved = {mask: swap(packed[mask], "dp", mask) for mask in ORDER}
        moved[0] = packed[0]
        received.append((first, count, [moved[mask] for mask in range(4)]))
        first += count
    results, sink_parts = [], []
    for first, count, packed in received:
        *grads, sink_part = attend(sink_logit, packed, first, count, heads_dev, score_scale)
        moved = {mask: swap(grads[mask], "dp", mask) for mask in ORDER}
        moved[0] = grads[0]
        results.append((first, [moved[mask] for mask in range(4)]))
        sink_parts.append(sink_part[:count])
    sink_term = -jnp.sum(jnp.concatenate(sink_parts, axis=0), axis=1)
    mask = 1
    while mask < lax.axis_size("ctx"):
        sink_term = sink_term + swap(sink_term, "ctx", mask)
        mask *= 2
    me = lax.axis_index("dp")
    sink_grad = jnp.zeros((4, heads_dev), jnp.float32)
    shares = {mask: swap(sink_term, "dp", mask) for mask in ORDER}
    shares[0] = sink_term
    for mask in range(4):
        sink_grad = lax.dynamic_update_slice(sink_grad, shares[mask][None], (me ^ mask, 0))
    outputs = ()
    for first, parts in results:
        outputs = unpack(parts, outputs, first * head_size, share, queries.shape)
    return (*outputs, sink_grad.reshape(heads))


def from_behind(value, axis, steps):
    count = lax.axis_size(axis)
    initial, last = (max(0, -steps), min(count, count - steps))
    return lax.ppermute(value, axis, [(source, source + steps) for source in range(initial, last)])


def causal_table(block_len):
    rows_iota = lax.broadcasted_iota(jnp.int32, (block_len, block_len), 0)
    cols_iota = lax.broadcasted_iota(jnp.int32, (block_len, block_len), 1)
    return rows_iota >= cols_iota


def attend_forward(q_blocks, key_all, val_all, allowed, sink_logit, score_scale):
    scores = (
        jnp.einsum("bqhd,bkhd->bhqk", q_blocks, key_all, preferred_element_type=jnp.float32)
        * score_scale
    )
    scores = jnp.where(allowed[:, None], scores, NEG_FILL)
    row_max = jnp.maximum(jnp.max(scores, axis=-1), sink_logit[None, :, None])
    exp_scores = jnp.exp(scores - row_max[..., None])
    sink_exp = jnp.exp(sink_logit[None, :, None] - row_max)
    denominator = jnp.sum(exp_scores, axis=-1) + sink_exp
    soft_prob = exp_scores / denominator[..., None]
    sink_prob = sink_exp / denominator
    weights = soft_prob.astype(jnp.bfloat16)
    output = jnp.einsum(
        "bhqk,bkhd->bqhd", weights, val_all, preferred_element_type=jnp.float32
    ).astype(jnp.bfloat16)
    return (soft_prob, weights, sink_prob, output)


def attend_backward(
    q_blocks, key_all, val_all, grad_blocks, soft_prob, weights, sink_prob, output, score_scale
):
    row_delta = jnp.sum(grad_blocks.astype(jnp.float32) * output.astype(jnp.float32), axis=-1)
    row_delta = jnp.transpose(row_delta, (0, 2, 1))
    prob_grad = jnp.einsum(
        "bqhd,bkhd->bhqk", grad_blocks, val_all, preferred_element_type=jnp.float32
    )
    score_grad = (soft_prob * (prob_grad - row_delta[..., None])).astype(jnp.bfloat16)
    query_grad = (
        jnp.einsum("bhqk,bkhd->bqhd", score_grad, key_all, preferred_element_type=jnp.float32)
        * score_scale
    ).astype(jnp.bfloat16)
    key_terms = (
        jnp.einsum("bhqk,bqhd->bkhd", score_grad, q_blocks, preferred_element_type=jnp.float32)
        * score_scale
    )
    value_terms = jnp.einsum(
        "bhqk,bqhd->bkhd", weights, grad_blocks, preferred_element_type=jnp.float32
    )
    sink_term = -jnp.sum(sink_prob * row_delta, axis=(0, 2))
    return (query_grad, key_terms, value_terms, sink_term)


def keys_travel_body(queries, key_states, values, out_grad, block_links, sink_logit):
    tokens = queries.shape[1]
    width = queries.shape[2]
    blocks = tokens // BLOCK
    heads = sink_logit.shape[0]
    head_size = width // heads
    score_scale = head_size ** (-0.5)

    def to_blocks(array):
        return array.reshape(blocks, BLOCK, heads, head_size)

    q_blocks = to_blocks(queries)
    grad_blocks = to_blocks(out_grad)
    level_live = block_links >= 0
    causal = jnp.broadcast_to(causal_table(BLOCK), (blocks, BLOCK, BLOCK))
    remote_masks = [
        jnp.broadcast_to(level_live[level_num][:, None, None], (blocks, BLOCK, BLOCK))
        for level_num in range(LEVELS)
    ]
    allowed = jnp.concatenate([causal] + remote_masks, axis=2)
    fetched = []
    for level_num in range(LEVELS):
        fetched.append(from_behind((key_states, values), "dp", 2**level_num))
    key_all = jnp.concatenate(
        [to_blocks(key_states)] + [to_blocks(moved[0]) for moved in fetched], axis=1
    )
    val_all = jnp.concatenate(
        [to_blocks(values)] + [to_blocks(moved[1]) for moved in fetched], axis=1
    )
    soft_prob, weights, sink_prob, output = attend_forward(
        q_blocks, key_all, val_all, allowed, sink_logit, score_scale
    )
    query_grad, key_terms, value_terms, sink_term = attend_backward(
        q_blocks, key_all, val_all, grad_blocks, soft_prob, weights, sink_prob, output, score_scale
    )
    key_grad = key_terms[:, :BLOCK].reshape(1, tokens, width)
    value_grad = value_terms[:, :BLOCK].reshape(1, tokens, width)
    for level_num in range(LEVELS):
        first_col = BLOCK * (1 + level_num)
        key_part = (
            key_terms[:, first_col : first_col + BLOCK]
            .reshape(1, tokens, width)
            .astype(jnp.bfloat16)
        )
        value_part = (
            value_terms[:, first_col : first_col + BLOCK]
            .reshape(1, tokens, width)
            .astype(jnp.bfloat16)
        )
        key_back, value_back = from_behind((key_part, value_part), "dp", -(2**level_num))
        key_grad = key_grad + key_back.astype(jnp.float32)
        value_grad = value_grad + value_back.astype(jnp.float32)
    sink_grad = lax.psum(sink_term, ("dp", "ctx"))
    return (
        query_grad.reshape(1, tokens, width),
        key_grad.astype(jnp.bfloat16),
        value_grad.astype(jnp.bfloat16),
        sink_grad,
    )


CHUNKS = (3, 2)


def body(queries, key_states, values, out_grad, block_links, sink_logit):
    heads = sink_logit.shape[0]
    blocks = lax.axis_size("dp")
    groups = lax.axis_size("ctx")
    fits = (
        blocks == 4
        and queries.shape[:2] == (1, BLOCK)
        and queries.shape[2] == heads * BLOCK
        and heads == 4 * sum(CHUNKS)
        and groups & (groups - 1) == 0
    )
    plan = functools.partial(head_shares_body, CHUNKS) if fits else keys_travel_body
    return plan(queries, key_states, values, out_grad, block_links, sink_logit)


def solution(mesh):
    placed = (
        P("ctx", "dp", None),
        P("ctx", "dp", None),
        P("ctx", "dp", None),
        P("ctx", "dp", None),
        P(None, "dp"),
        P(),
    )
    return jax.shard_map(
        body,
        mesh=mesh,
        in_specs=placed,
        out_specs=(P("ctx", "dp", None), P("ctx", "dp", None), P("ctx", "dp", None), P()),
        check_vma=False,
    )
```

```python
import functools

import jax
import jax.numpy as jnp
from jax import lax
from jax.experimental import pallas as pl
from jax.experimental.pallas import tpu as pltpu
from jax.sharding import PartitionSpec as P

BLOCK = 128
LEVELS = 2
FLAG_ROWS = 16
LOG2_E = 1.4426950408889634
NEG_FILL = -1e30
ORDER = (3, 1, 2)


def pack_kernel(offset, width, share, links, *refs):
    arrays, outs, (held, load_sems, store_sems) = refs[:4], refs[4:7], refs[7:]
    me = lax.axis_index("dp")
    loads, stores = [], []
    for place, mask in enumerate(ORDER):
        start = pl.multiple_of((me ^ mask) * share + offset, BLOCK)
        loads.append(
            [
                pltpu.make_async_copy(
                    array.at[0, :, pl.ds(start, width)],
                    held.at[place, pl.ds(num * BLOCK, BLOCK), :],
                    load_sems.at[place, num],
                )
                for num, array in enumerate(arrays)
            ]
        )
        for copy in loads[-1]:
            copy.start()
    flags = live_flags(links, width)
    for place in range(3):
        held[place, 4 * BLOCK :, :] = flags
    for place in range(3):
        for copy in loads[place]:
            copy.wait()
        stores.append(pltpu.make_async_copy(held.at[place], outs[place], store_sems.at[place]))
        stores[-1].start()
    for copy in stores:
        copy.wait()


def live_flags(links, width):
    live = [jnp.where(links[level] >= 0, 1.0, 0.0) for level in range(LEVELS)]
    row = lax.broadcasted_iota(jnp.int32, (FLAG_ROWS, width), 0)
    return jnp.where(row < 8, live[0], live[1]).astype(jnp.bfloat16)


def pack(links, arrays, offset, width, share):
    rows = 4 * BLOCK + FLAG_ROWS
    return pl.pallas_call(
        functools.partial(pack_kernel, offset, width, share),
        out_shape=[jax.ShapeDtypeStruct((rows, width), jnp.bfloat16)] * 3,
        in_specs=[pl.BlockSpec(memory_space=pltpu.SMEM)] + [pl.BlockSpec(memory_space=pl.ANY)] * 4,
        out_specs=[pl.BlockSpec(memory_space=pl.ANY)] * 3,
        scratch_shapes=[
            pltpu.VMEM((3, rows, width), jnp.bfloat16),
            pltpu.SemaphoreType.DMA((3, 4)),
            pltpu.SemaphoreType.DMA((3,)),
        ],
        cost_estimate=pl.CostEstimate(flops=0, bytes_accessed=12 * rows * width, transcendentals=0),
        name="pack",
    )(links, *arrays)


def dot_nt(a, b):
    return lax.dot_general(a, b, (((1,), (1,)), ((), ())), preferred_element_type=jnp.float32)


def dot_nn(a, b):
    return lax.dot_general(a, b, (((1,), (0,)), ((), ())), preferred_element_type=jnp.float32)


def dot_tn(a, b):
    return lax.dot_general(a, b, (((0,), (0,)), ((), ())), preferred_element_type=jnp.float32)


def attend_kernel(first_head, heads, heads_dev, score_scale, num_previous, sink, links, sink_in, *refs):
    arrays, ins, refs = refs[:4], refs[4:7], refs[7 + num_previous :]
    outs, own_outs, sink_out = refs[:3], refs[3:6], refs[6]
    held, grads, own_sems, in_sems, own_out_sems, out_sems = refs[7:]
    me = lax.axis_index("dp")
    blocks = 4

    def own_columns(head):
        return pl.ds(pl.multiple_of((me * heads_dev + first_head + head) * BLOCK, BLOCK), BLOCK)

    def columns(head):
        return pl.ds(head * BLOCK, BLOCK)

    loads = [
        [
            pltpu.make_async_copy(
                array.at[0, :, own_columns(head)],
                held.at[me, pl.ds(num * BLOCK, BLOCK), columns(head)],
                own_sems.at[head, num],
            )
            for num, array in enumerate(arrays)
        ]
        + [
            pltpu.make_async_copy(
                ins[place].at[:, columns(head)],
                held.at[me ^ mask, :, columns(head)],
                in_sems.at[head, place],
            )
            for place, mask in enumerate(ORDER)
        ]
        for head in range(heads)
    ]
    for group in loads:
        for copy in group:
            copy.start()
    held[me, 4 * BLOCK :, :] = live_flags(links, held.shape[2])
    keys_iota = lax.broadcasted_iota(jnp.int32, (BLOCK, BLOCK), 0)
    queries_iota = lax.broadcasted_iota(jnp.int32, (BLOCK, BLOCK), 1)
    causal = keys_iota <= queries_iota
    lanes = lax.broadcasted_iota(jnp.int32, (8, BLOCK), 1)
    sink_sum = sink_in[...]
    stores = []
    for head in range(heads):
        for copy in loads[head]:
            copy.wait()
        cols = columns(head)

        def part(kind, first, last):
            return held[first : last + 1, kind * BLOCK : (kind + 1) * BLOCK, cols].reshape(
                (last + 1 - first) * BLOCK, BLOCK
            )

        sink_logit = sink[me * heads_dev + first_head + head] * LOG2_E
        scores, prob_grads = {}, {}
        for pair in range(0, blocks, 2):
            first = max(0, pair - LEVELS)
            score = dot_nt(part(1, first, pair + 1), part(0, pair, pair + 1))
            prob_grad = dot_nt(part(2, first, pair + 1), part(3, pair, pair + 1))
            for block in (pair, pair + 1):
                lanes_here = slice((block - pair) * BLOCK, (block - pair + 1) * BLOCK)
                for source in range(max(0, block - LEVELS), block + 1):
                    rows = slice((source - first) * BLOCK, (source - first + 1) * BLOCK)
                    scores[block, source] = score[rows, lanes_here]
                    prob_grads[block, source] = prob_grad[rows, lanes_here]
        sink_total = jnp.zeros((1, BLOCK), jnp.float32)
        weights, score_grads = {}, {}
        for block in range(blocks):
            sources = range(max(0, block - LEVELS), block + 1)
            flags = held[block, 4 * BLOCK :, cols].astype(jnp.float32)
            pieces = []
            for source in sources:
                piece = scores[block, source] * (score_scale * LOG2_E)
                if source == block:
                    piece = jnp.where(causal, piece, NEG_FILL)
                else:
                    row = 8 * (block - source - 1)
                    piece = jnp.where(flags[row : row + 1] > 0.5, piece, NEG_FILL)
                pieces.append(piece)
            row_max = functools.reduce(jnp.maximum, pieces)
            row_max = jnp.maximum(jnp.max(row_max, axis=0, keepdims=True), sink_logit)
            pieces = [jnp.exp2(piece - row_max) for piece in pieces]
            sink_exp = jnp.exp2(sink_logit - row_max)
            denominator = jnp.sum(functools.reduce(jnp.add, pieces), axis=0, keepdims=True) + sink_exp
            scale = 1.0 / denominator
            pieces = [piece * scale for piece in pieces]
            products = [piece * prob_grads[block, source] for piece, source in zip(pieces, sources)]
            row_delta = jnp.sum(functools.reduce(jnp.add, products), axis=0, keepdims=True)
            sink_total = sink_total + sink_exp * scale * row_delta
            for piece, source in zip(pieces, sources):
                weights[block, source] = piece.astype(jnp.bfloat16)
                score_grads[block, source] = (
                    piece * (prob_grads[block, source] - row_delta)
                ).astype(jnp.bfloat16)
        here = lanes == me * heads_dev + first_head + head
        sink_sum = sink_sum - jnp.where(here, jnp.sum(sink_total, axis=1, keepdims=True), 0.0)
        for block in range(blocks):
            first = max(0, block - LEVELS)
            score_grad = jnp.concatenate([score_grads[block, b] for b in range(first, block + 1)], axis=0)
            query_grad = dot_tn(score_grad, part(1, first, block)) * score_scale
            grads[block, 0:BLOCK, cols] = query_grad.astype(jnp.bfloat16)
        for source in range(blocks):
            last = min(blocks - 1, source + LEVELS)
            score_grad = jnp.concatenate([score_grads[b, source] for b in range(source, last + 1)], axis=1)
            weight = jnp.concatenate([weights[b, source] for b in range(source, last + 1)], axis=1)
            key_grad = dot_nn(score_grad, part(0, source, last)) * score_scale
            value_grad = dot_nn(weight, part(3, source, last))
            grads[source, BLOCK : 2 * BLOCK, cols] = key_grad.astype(jnp.bfloat16)
            grads[source, 2 * BLOCK : 3 * BLOCK, cols] = value_grad.astype(jnp.bfloat16)
        copies = [
            pltpu.make_async_copy(
                grads.at[me ^ mask, :, cols], outs[place].at[:, cols], out_sems.at[head, place]
            )
            for place, mask in enumerate(ORDER)
        ] + [
            pltpu.make_async_copy(
                grads.at[me, pl.ds(num * BLOCK, BLOCK), cols],
                out.at[0, :, own_columns(head)],
                own_out_sems.at[head, num],
            )
            for num, out in enumerate(own_outs)
        ]
        for copy in copies:
            copy.start()
        stores.extend(copies)
    sink_out[...] = sink_sum
    for copy in stores:
        copy.wait()


def attend(sink_logit, links, sink_sum, arrays, packed, previous, first_head, heads, heads_dev, score_scale):
    rows, width = packed[0].shape
    grad_rows = 3 * BLOCK
    hbm = pl.BlockSpec(memory_space=pl.ANY)
    smem = pl.BlockSpec(memory_space=pltpu.SMEM)
    vmem = pl.BlockSpec(memory_space=pltpu.VMEM)
    return pl.pallas_call(
        functools.partial(attend_kernel, first_head, heads, heads_dev, score_scale, len(previous)),
        out_shape=[jax.ShapeDtypeStruct((grad_rows, width), jnp.bfloat16)] * 3
        + [jax.ShapeDtypeStruct(arrays[0].shape, jnp.bfloat16)] * 3
        + [jax.ShapeDtypeStruct((8, BLOCK), jnp.float32)],
        in_specs=[smem, smem, vmem] + [hbm] * (7 + len(previous)),
        out_specs=[hbm] * 6 + [vmem],
        scratch_shapes=[
            pltpu.VMEM((4, rows, width), jnp.bfloat16),
            pltpu.VMEM((4, grad_rows, width), jnp.bfloat16),
            pltpu.SemaphoreType.DMA((heads, 4)),
            pltpu.SemaphoreType.DMA((heads, 3)),
            pltpu.SemaphoreType.DMA((heads, 3)),
            pltpu.SemaphoreType.DMA((heads, 3)),
        ],
        input_output_aliases={10 + num: 3 + num for num in range(len(previous))},
        compiler_params=pltpu.CompilerParams(vmem_limit_bytes=32 * 2**20),
        cost_estimate=pl.CostEstimate(flops=0, bytes_accessed=0, transcendentals=0),
        name="attend",
    )(sink_logit, links, sink_sum, *arrays, *packed, *previous)


def unpack_kernel(offset, width, share, *refs):
    ins, outs, sems = refs[:3], refs[6:9], refs[9]
    me = lax.axis_index("dp")
    copies = []
    for place, mask in enumerate(ORDER):
        start = pl.multiple_of((me ^ mask) * share + offset, BLOCK)
        for num, out in enumerate(outs):
            copies.append(
                pltpu.make_async_copy(
                    ins[place].at[pl.ds(num * BLOCK, BLOCK), :],
                    out.at[0, :, pl.ds(start, width)],
                    sems.at[place, num],
                )
            )
    for copy in copies:
        copy.start()
    for copy in copies:
        copy.wait()


def unpack(parts, previous, offset, share):
    width = parts[0].shape[1]
    return pl.pallas_call(
        functools.partial(unpack_kernel, offset, width, share),
        out_shape=[jax.ShapeDtypeStruct(out.shape, out.dtype) for out in previous],
        in_specs=[pl.BlockSpec(memory_space=pltpu.VMEM)] * 3 + [pl.BlockSpec(memory_space=pl.ANY)] * 3,
        out_specs=[pl.BlockSpec(memory_space=pl.ANY)] * 3,
        scratch_shapes=[pltpu.SemaphoreType.DMA((3, 3))],
        input_output_aliases={3 + num: num for num in range(3)},
        cost_estimate=pl.CostEstimate(flops=0, bytes_accessed=8 * 3 * BLOCK * width, transcendentals=0),
        name="unpack",
    )(*parts, *previous)


def swap(value, axis, mask):
    return lax.ppermute(value, axis, [(i, i ^ mask) for i in range(lax.axis_size(axis))])


def after(value, other):
    return lax.optimization_barrier((value, other))


def butterfly(value, axis):
    mask = 1
    while mask < lax.axis_size(axis):
        value = value + swap(value, axis, mask)
        mask *= 2
    return value


def head_shares_body(chunks, queries, key_states, values, out_grad, block_links, sink_logit):
    heads = sink_logit.shape[0]
    head_size = queries.shape[2] // heads
    score_scale = head_size ** (-0.5)
    heads_dev = heads // 4
    share = heads_dev * head_size
    arrays = (queries, key_states, values, out_grad)
    links = block_links.reshape(LEVELS)
    received, first = [], 0
    for count in chunks:
        packed = list(pack(links, arrays, first * head_size, count * head_size, share))
        moved = [None] * 3
        for place, mask in enumerate(ORDER):
            if received:
                packed[place], received[-1][2][place] = after(packed[place], received[-1][2][place])
            moved[place] = swap(packed[place], "dp", mask)
        received.append((first, count, moved))
        first += count
    results, outputs, sink_sum = [], [], jnp.zeros((8, BLOCK), jnp.float32)
    for num, (first, count, packed) in enumerate(received):
        *grads, sink_sum = attend(
            sink_logit, links, sink_sum, arrays, packed, outputs, first, count, heads_dev, score_scale
        )
        grads, outputs = grads[:3], grads[3:]
        moved = [None] * 3
        for place, mask in enumerate(ORDER):
            if num:
                grads[place], results[-1][1][place] = after(grads[place], results[-1][1][place])
            else:
                grads[place], received[1][2][0] = after(grads[place], received[1][2][0])
            moved[place] = swap(grads[place], "dp", mask)
        results.append((first, moved))
    sink_sum, results[0][1][0] = after(sink_sum, results[0][1][0])
    once = jnp.minimum(links[0] + 2, 1)
    sink_sum = lax.fori_loop(0, once, lambda _, held: butterfly(held, "ctx"), sink_sum)
    sink_sum = butterfly(sink_sum, "dp")
    for first, parts in results:
        outputs = unpack(parts, outputs, first * head_size, share)
    return (*outputs, sink_sum[0, :heads])


def from_behind(value, axis, steps):
    count = lax.axis_size(axis)
    initial, last = (max(0, -steps), min(count, count - steps))
    return lax.ppermute(value, axis, [(source, source + steps) for source in range(initial, last)])


def causal_table(block_len):
    rows_iota = lax.broadcasted_iota(jnp.int32, (block_len, block_len), 0)
    cols_iota = lax.broadcasted_iota(jnp.int32, (block_len, block_len), 1)
    return rows_iota >= cols_iota


def attend_forward(q_blocks, key_all, val_all, allowed, sink_logit, score_scale):
    scores = (
        jnp.einsum("bqhd,bkhd->bhqk", q_blocks, key_all, preferred_element_type=jnp.float32)
        * score_scale
    )
    scores = jnp.where(allowed[:, None], scores, NEG_FILL)
    row_max = jnp.maximum(jnp.max(scores, axis=-1), sink_logit[None, :, None])
    exp_scores = jnp.exp(scores - row_max[..., None])
    sink_exp = jnp.exp(sink_logit[None, :, None] - row_max)
    denominator = jnp.sum(exp_scores, axis=-1) + sink_exp
    soft_prob = exp_scores / denominator[..., None]
    sink_prob = sink_exp / denominator
    weights = soft_prob.astype(jnp.bfloat16)
    output = jnp.einsum(
        "bhqk,bkhd->bqhd", weights, val_all, preferred_element_type=jnp.float32
    ).astype(jnp.bfloat16)
    return (soft_prob, weights, sink_prob, output)


def attend_backward(
    q_blocks, key_all, val_all, grad_blocks, soft_prob, weights, sink_prob, output, score_scale
):
    row_delta = jnp.sum(grad_blocks.astype(jnp.float32) * output.astype(jnp.float32), axis=-1)
    row_delta = jnp.transpose(row_delta, (0, 2, 1))
    prob_grad = jnp.einsum(
        "bqhd,bkhd->bhqk", grad_blocks, val_all, preferred_element_type=jnp.float32
    )
    score_grad = (soft_prob * (prob_grad - row_delta[..., None])).astype(jnp.bfloat16)
    query_grad = (
        jnp.einsum("bhqk,bkhd->bqhd", score_grad, key_all, preferred_element_type=jnp.float32)
        * score_scale
    ).astype(jnp.bfloat16)
    key_terms = (
        jnp.einsum("bhqk,bqhd->bkhd", score_grad, q_blocks, preferred_element_type=jnp.float32)
        * score_scale
    )
    value_terms = jnp.einsum(
        "bhqk,bqhd->bkhd", weights, grad_blocks, preferred_element_type=jnp.float32
    )
    sink_term = -jnp.sum(sink_prob * row_delta, axis=(0, 2))
    return (query_grad, key_terms, value_terms, sink_term)


def keys_travel_body(queries, key_states, values, out_grad, block_links, sink_logit):
    tokens = queries.shape[1]
    width = queries.shape[2]
    blocks = tokens // BLOCK
    heads = sink_logit.shape[0]
    head_size = width // heads
    score_scale = head_size ** (-0.5)

    def to_blocks(array):
        return array.reshape(blocks, BLOCK, heads, head_size)

    q_blocks = to_blocks(queries)
    grad_blocks = to_blocks(out_grad)
    level_live = block_links >= 0
    causal = jnp.broadcast_to(causal_table(BLOCK), (blocks, BLOCK, BLOCK))
    remote_masks = [
        jnp.broadcast_to(level_live[level_num][:, None, None], (blocks, BLOCK, BLOCK))
        for level_num in range(LEVELS)
    ]
    allowed = jnp.concatenate([causal] + remote_masks, axis=2)
    fetched = []
    for level_num in range(LEVELS):
        fetched.append(from_behind((key_states, values), "dp", 2**level_num))
    key_all = jnp.concatenate(
        [to_blocks(key_states)] + [to_blocks(moved[0]) for moved in fetched], axis=1
    )
    val_all = jnp.concatenate(
        [to_blocks(values)] + [to_blocks(moved[1]) for moved in fetched], axis=1
    )
    soft_prob, weights, sink_prob, output = attend_forward(
        q_blocks, key_all, val_all, allowed, sink_logit, score_scale
    )
    query_grad, key_terms, value_terms, sink_term = attend_backward(
        q_blocks, key_all, val_all, grad_blocks, soft_prob, weights, sink_prob, output, score_scale
    )
    key_grad = key_terms[:, :BLOCK].reshape(1, tokens, width)
    value_grad = value_terms[:, :BLOCK].reshape(1, tokens, width)
    for level_num in range(LEVELS):
        first_col = BLOCK * (1 + level_num)
        key_part = (
            key_terms[:, first_col : first_col + BLOCK]
            .reshape(1, tokens, width)
            .astype(jnp.bfloat16)
        )
        value_part = (
            value_terms[:, first_col : first_col + BLOCK]
            .reshape(1, tokens, width)
            .astype(jnp.bfloat16)
        )
        key_back, value_back = from_behind((key_part, value_part), "dp", -(2**level_num))
        key_grad = key_grad + key_back.astype(jnp.float32)
        value_grad = value_grad + value_back.astype(jnp.float32)
    sink_grad = lax.psum(sink_term, ("dp", "ctx"))
    return (
        query_grad.reshape(1, tokens, width),
        key_grad.astype(jnp.bfloat16),
        value_grad.astype(jnp.bfloat16),
        sink_grad,
    )


CHUNKS = (2, 3)


def body(queries, key_states, values, out_grad, block_links, sink_logit):
    heads = sink_logit.shape[0]
    blocks = lax.axis_size("dp")
    groups = lax.axis_size("ctx")
    fits = (
        blocks == 4
        and queries.shape[:2] == (1, BLOCK)
        and queries.shape[2] == heads * BLOCK
        and heads == 4 * sum(CHUNKS)
        and groups & (groups - 1) == 0
    )
    plan = functools.partial(head_shares_body, CHUNKS) if fits else keys_travel_body
    return plan(queries, key_states, values, out_grad, block_links, sink_logit)


def solution(mesh):
    placed = (
        P("ctx", "dp", None),
        P("ctx", "dp", None),
        P("ctx", "dp", None),
        P("ctx", "dp", None),
        P(None, "dp"),
        P(),
    )
    return jax.shard_map(
        body,
        mesh=mesh,
        in_specs=placed,
        out_specs=(P("ctx", "dp", None), P("ctx", "dp", None), P("ctx", "dp", None), P()),
        check_vma=False,
    )
```

```python
import functools

import jax
import jax.numpy as jnp
from jax import lax
from jax.experimental import pallas as pl
from jax.experimental.pallas import tpu as pltpu
from jax.sharding import PartitionSpec as P

BLOCK = 128
LEVELS = 2
FLAG_ROWS = 16
LOG2_E = 1.4426950408889634
NEG_FILL = -1e30
ORDER = (3, 1, 2)


def pack_kernel(offset, width, share, links, *refs):
    arrays, outs, (held, load_sems, store_sems) = refs[:4], refs[4:7], refs[7:]
    me = lax.axis_index("dp")
    loads, stores = [], []
    for place, mask in enumerate(ORDER):
        start = pl.multiple_of((me ^ mask) * share + offset, BLOCK)
        loads.append(
            [
                pltpu.make_async_copy(
                    array.at[0, :, pl.ds(start, width)],
                    held.at[place, pl.ds(num * BLOCK, BLOCK), :],
                    load_sems.at[place, num],
                )
                for num, array in enumerate(arrays)
            ]
        )
        for copy in loads[-1]:
            copy.start()
    flags = live_flags(links, width)
    for place in range(3):
        held[place, 4 * BLOCK :, :] = flags
    for place in range(3):
        for copy in loads[place]:
            copy.wait()
        stores.append(pltpu.make_async_copy(held.at[place], outs[place], store_sems.at[place]))
        stores[-1].start()
    for copy in stores:
        copy.wait()


def live_flags(links, width):
    live = [jnp.where(links[level] >= 0, 1.0, 0.0) for level in range(LEVELS)]
    row = lax.broadcasted_iota(jnp.int32, (FLAG_ROWS, width), 0)
    return jnp.where(row < 8, live[0], live[1]).astype(jnp.bfloat16)


def pack(links, arrays, offset, width, share):
    rows = 4 * BLOCK + FLAG_ROWS
    return pl.pallas_call(
        functools.partial(pack_kernel, offset, width, share),
        out_shape=[jax.ShapeDtypeStruct((rows, width), jnp.bfloat16)] * 3,
        in_specs=[pl.BlockSpec(memory_space=pltpu.SMEM)] + [pl.BlockSpec(memory_space=pl.ANY)] * 4,
        out_specs=[pl.BlockSpec(memory_space=pl.ANY)] * 3,
        scratch_shapes=[
            pltpu.VMEM((3, rows, width), jnp.bfloat16),
            pltpu.SemaphoreType.DMA((3, 4)),
            pltpu.SemaphoreType.DMA((3,)),
        ],
        cost_estimate=pl.CostEstimate(flops=0, bytes_accessed=12 * rows * width, transcendentals=0),
        name="pack",
    )(links, *arrays)


def dot_nt(a, b):
    return lax.dot_general(a, b, (((1,), (1,)), ((), ())), preferred_element_type=jnp.float32)


def dot_nn(a, b):
    return lax.dot_general(a, b, (((1,), (0,)), ((), ())), preferred_element_type=jnp.float32)


def dot_tn(a, b):
    return lax.dot_general(a, b, (((0,), (0,)), ((), ())), preferred_element_type=jnp.float32)


def attend_kernel(first_head, heads, heads_dev, score_scale, num_previous, sink, links, sink_in, *refs):
    arrays, ins, refs = refs[:4], refs[4:7], refs[7 + num_previous :]
    outs, own_outs, sink_out = refs[:3], refs[3:6], refs[6]
    held, grads, own_sems, in_sems, own_out_sems, out_sems = refs[7:]
    me = lax.axis_index("dp")
    blocks = 4

    def own_columns(head):
        return pl.ds(pl.multiple_of((me * heads_dev + first_head + head) * BLOCK, BLOCK), BLOCK)

    def columns(head):
        return pl.ds(head * BLOCK, BLOCK)

    loads = [
        [
            pltpu.make_async_copy(
                array.at[0, :, own_columns(head)],
                held.at[me, pl.ds(num * BLOCK, BLOCK), columns(head)],
                own_sems.at[head, num],
            )
            for num, array in enumerate(arrays)
        ]
        + [
            pltpu.make_async_copy(
                ins[place].at[:, columns(head)],
                held.at[me ^ mask, :, columns(head)],
                in_sems.at[head, place],
            )
            for place, mask in enumerate(ORDER)
        ]
        for head in range(heads)
    ]
    for group in loads:
        for copy in group:
            copy.start()
    held[me, 4 * BLOCK :, :] = live_flags(links, held.shape[2])
    keys_iota = lax.broadcasted_iota(jnp.int32, (BLOCK, BLOCK), 0)
    queries_iota = lax.broadcasted_iota(jnp.int32, (BLOCK, BLOCK), 1)
    causal = keys_iota <= queries_iota
    lanes = lax.broadcasted_iota(jnp.int32, (8, BLOCK), 1)
    sink_sum = sink_in[...]
    stores = []
    for head in range(heads):
        for copy in loads[head]:
            copy.wait()
        cols = columns(head)

        def part(kind, first, last):
            return held[first : last + 1, kind * BLOCK : (kind + 1) * BLOCK, cols].reshape(
                (last + 1 - first) * BLOCK, BLOCK
            )

        sink_logit = sink[me * heads_dev + first_head + head] * LOG2_E
        scores, prob_grads = {}, {}
        for pair in range(0, blocks, 2):
            first = max(0, pair - LEVELS)
            score = dot_nt(part(1, first, pair + 1), part(0, pair, pair + 1))
            prob_grad = dot_nt(part(2, first, pair + 1), part(3, pair, pair + 1))
            for block in (pair, pair + 1):
                lanes_here = slice((block - pair) * BLOCK, (block - pair + 1) * BLOCK)
                for source in range(max(0, block - LEVELS), block + 1):
                    rows = slice((source - first) * BLOCK, (source - first + 1) * BLOCK)
                    scores[block, source] = score[rows, lanes_here]
                    prob_grads[block, source] = prob_grad[rows, lanes_here]
        sink_total = jnp.zeros((1, BLOCK), jnp.float32)
        weights, score_grads = {}, {}
        for block in range(blocks):
            sources = range(max(0, block - LEVELS), block + 1)
            flags = held[block, 4 * BLOCK :, cols].astype(jnp.float32)
            pieces = []
            for source in sources:
                piece = scores[block, source] * (score_scale * LOG2_E)
                if source == block:
                    piece = jnp.where(causal, piece, NEG_FILL)
                else:
                    row = 8 * (block - source - 1)
                    piece = jnp.where(flags[row : row + 1] > 0.5, piece, NEG_FILL)
                pieces.append(piece)
            row_max = functools.reduce(jnp.maximum, pieces)
            row_max = jnp.maximum(jnp.max(row_max, axis=0, keepdims=True), sink_logit)
            pieces = [jnp.exp2(piece - row_max) for piece in pieces]
            sink_exp = jnp.exp2(sink_logit - row_max)
            denominator = jnp.sum(functools.reduce(jnp.add, pieces), axis=0, keepdims=True) + sink_exp
            scale = 1.0 / denominator
            pieces = [piece * scale for piece in pieces]
            products = [piece * prob_grads[block, source] for piece, source in zip(pieces, sources)]
            row_delta = jnp.sum(functools.reduce(jnp.add, products), axis=0, keepdims=True)
            sink_total = sink_total + sink_exp * scale * row_delta
            for piece, source in zip(pieces, sources):
                weights[block, source] = piece.astype(jnp.bfloat16)
                score_grads[block, source] = (
                    piece * (prob_grads[block, source] - row_delta)
                ).astype(jnp.bfloat16)
        here = lanes == me * heads_dev + first_head + head
        sink_sum = sink_sum - jnp.where(here, jnp.sum(sink_total, axis=1, keepdims=True), 0.0)
        for block in range(blocks):
            first = max(0, block - LEVELS)
            score_grad = jnp.concatenate([score_grads[block, b] for b in range(first, block + 1)], axis=0)
            query_grad = dot_tn(score_grad, part(1, first, block)) * score_scale
            grads[block, 0:BLOCK, cols] = query_grad.astype(jnp.bfloat16)
        for source in range(blocks):
            last = min(blocks - 1, source + LEVELS)
            score_grad = jnp.concatenate([score_grads[b, source] for b in range(source, last + 1)], axis=1)
            weight = jnp.concatenate([weights[b, source] for b in range(source, last + 1)], axis=1)
            key_grad = dot_nn(score_grad, part(0, source, last)) * score_scale
            value_grad = dot_nn(weight, part(3, source, last))
            grads[source, BLOCK : 2 * BLOCK, cols] = key_grad.astype(jnp.bfloat16)
            grads[source, 2 * BLOCK : 3 * BLOCK, cols] = value_grad.astype(jnp.bfloat16)
        copies = [
            pltpu.make_async_copy(
                grads.at[me ^ mask, :, cols], outs[place].at[:, cols], out_sems.at[head, place]
            )
            for place, mask in enumerate(ORDER)
        ] + [
            pltpu.make_async_copy(
                grads.at[me, pl.ds(num * BLOCK, BLOCK), cols],
                out.at[0, :, own_columns(head)],
                own_out_sems.at[head, num],
            )
            for num, out in enumerate(own_outs)
        ]
        for copy in copies:
            copy.start()
        stores.extend(copies)
    sink_out[...] = sink_sum
    for copy in stores:
        copy.wait()


def attend(sink_logit, links, sink_sum, arrays, packed, previous, first_head, heads, heads_dev, score_scale):
    rows, width = packed[0].shape
    grad_rows = 3 * BLOCK
    hbm = pl.BlockSpec(memory_space=pl.ANY)
    smem = pl.BlockSpec(memory_space=pltpu.SMEM)
    vmem = pl.BlockSpec(memory_space=pltpu.VMEM)
    return pl.pallas_call(
        functools.partial(attend_kernel, first_head, heads, heads_dev, score_scale, len(previous)),
        out_shape=[jax.ShapeDtypeStruct((grad_rows, width), jnp.bfloat16)] * 3
        + [jax.ShapeDtypeStruct(arrays[0].shape, jnp.bfloat16)] * 3
        + [jax.ShapeDtypeStruct((8, BLOCK), jnp.float32)],
        in_specs=[smem, smem, vmem] + [hbm] * (7 + len(previous)),
        out_specs=[hbm] * 6 + [vmem],
        scratch_shapes=[
            pltpu.VMEM((4, rows, width), jnp.bfloat16),
            pltpu.VMEM((4, grad_rows, width), jnp.bfloat16),
            pltpu.SemaphoreType.DMA((heads, 4)),
            pltpu.SemaphoreType.DMA((heads, 3)),
            pltpu.SemaphoreType.DMA((heads, 3)),
            pltpu.SemaphoreType.DMA((heads, 3)),
        ],
        input_output_aliases={10 + num: 3 + num for num in range(len(previous))},
        compiler_params=pltpu.CompilerParams(vmem_limit_bytes=8 * 2**20),
        cost_estimate=pl.CostEstimate(flops=0, bytes_accessed=0, transcendentals=0),
        name="attend",
    )(sink_logit, links, sink_sum, *arrays, *packed, *previous)


def unpack_kernel(offset, width, share, *refs):
    ins, outs, (held, load_sems, store_sems) = refs[:3], refs[6:9], refs[9:]
    me = lax.axis_index("dp")
    loads = [
        pltpu.make_async_copy(ins[place], held.at[place], load_sems.at[place]) for place in range(3)
    ]
    for copy in loads:
        copy.start()
    stores = []
    for place, mask in enumerate(ORDER):
        loads[place].wait()
        start = pl.multiple_of((me ^ mask) * share + offset, BLOCK)
        for num, out in enumerate(outs):
            stores.append(
                pltpu.make_async_copy(
                    held.at[place, pl.ds(num * BLOCK, BLOCK), :],
                    out.at[0, :, pl.ds(start, width)],
                    store_sems.at[place, num],
                )
            )
            stores[-1].start()
    for copy in stores:
        copy.wait()


def unpack(parts, previous, offset, share):
    rows, width = parts[0].shape
    return pl.pallas_call(
        functools.partial(unpack_kernel, offset, width, share),
        out_shape=[jax.ShapeDtypeStruct(out.shape, out.dtype) for out in previous],
        in_specs=[pl.BlockSpec(memory_space=pl.ANY)] * 6,
        out_specs=[pl.BlockSpec(memory_space=pl.ANY)] * 3,
        scratch_shapes=[
            pltpu.VMEM((3, rows, width), jnp.bfloat16),
            pltpu.SemaphoreType.DMA((3,)),
            pltpu.SemaphoreType.DMA((3, 3)),
        ],
        input_output_aliases={3 + num: num for num in range(3)},
        compiler_params=pltpu.CompilerParams(vmem_limit_bytes=8 * 2**20),
        cost_estimate=pl.CostEstimate(flops=0, bytes_accessed=0, transcendentals=0),
        name="unpack",
    )(*parts, *previous)


def swap(value, axis, mask):
    return lax.ppermute(value, axis, [(i, i ^ mask) for i in range(lax.axis_size(axis))])


def after(value, other):
    return lax.optimization_barrier((value, other))


def butterfly(value, axis):
    mask = 1
    while mask < lax.axis_size(axis):
        value = value + swap(value, axis, mask)
        mask *= 2
    return value


def head_shares_body(chunks, queries, key_states, values, out_grad, block_links, sink_logit):
    heads = sink_logit.shape[0]
    head_size = queries.shape[2] // heads
    score_scale = head_size ** (-0.5)
    heads_dev = heads // 4
    share = heads_dev * head_size
    arrays = (queries, key_states, values, out_grad)
    links = block_links.reshape(LEVELS)
    received, first = [], 0
    for count in chunks:
        packed = pack(links, arrays, first * head_size, count * head_size, share)
        moved = [swap(part, "dp", mask) for part, mask in zip(packed, ORDER)]
        received.append((first, count, moved))
        first += count
    results, outputs, sink_sum = [], [], jnp.zeros((8, BLOCK), jnp.float32)
    for num, (first, count, packed) in enumerate(received):
        *grads, sink_sum = attend(
            sink_logit, links, sink_sum, arrays, packed, outputs, first, count, heads_dev, score_scale
        )
        grads, outputs = grads[:3], grads[3:]
        if num:
            grads[0], results[0][1][0] = after(grads[0], results[0][1][0])
        else:
            for place in (1, 2):
                grads[place], received[1][2][0] = after(grads[place], received[1][2][0])
        results.append((first, [swap(grad, "dp", mask) for grad, mask in zip(grads, ORDER)]))
    sink_sum, results[0][1][2] = after(sink_sum, results[0][1][2])
    once = jnp.minimum(links[0] + 2, 1)
    sink_sum = lax.fori_loop(0, once, lambda _, held: butterfly(held, "ctx"), sink_sum)
    sink_sum = butterfly(sink_sum, "dp")
    for first, parts in results:
        outputs = unpack(parts, outputs, first * head_size, share)
    return (*outputs, sink_sum[0, :heads])


def from_behind(value, axis, steps):
    count = lax.axis_size(axis)
    initial, last = (max(0, -steps), min(count, count - steps))
    return lax.ppermute(value, axis, [(source, source + steps) for source in range(initial, last)])


def causal_table(block_len):
    rows_iota = lax.broadcasted_iota(jnp.int32, (block_len, block_len), 0)
    cols_iota = lax.broadcasted_iota(jnp.int32, (block_len, block_len), 1)
    return rows_iota >= cols_iota


def attend_forward(q_blocks, key_all, val_all, allowed, sink_logit, score_scale):
    scores = (
        jnp.einsum("bqhd,bkhd->bhqk", q_blocks, key_all, preferred_element_type=jnp.float32)
        * score_scale
    )
    scores = jnp.where(allowed[:, None], scores, NEG_FILL)
    row_max = jnp.maximum(jnp.max(scores, axis=-1), sink_logit[None, :, None])
    exp_scores = jnp.exp(scores - row_max[..., None])
    sink_exp = jnp.exp(sink_logit[None, :, None] - row_max)
    denominator = jnp.sum(exp_scores, axis=-1) + sink_exp
    soft_prob = exp_scores / denominator[..., None]
    sink_prob = sink_exp / denominator
    weights = soft_prob.astype(jnp.bfloat16)
    output = jnp.einsum(
        "bhqk,bkhd->bqhd", weights, val_all, preferred_element_type=jnp.float32
    ).astype(jnp.bfloat16)
    return (soft_prob, weights, sink_prob, output)


def attend_backward(
    q_blocks, key_all, val_all, grad_blocks, soft_prob, weights, sink_prob, output, score_scale
):
    row_delta = jnp.sum(grad_blocks.astype(jnp.float32) * output.astype(jnp.float32), axis=-1)
    row_delta = jnp.transpose(row_delta, (0, 2, 1))
    prob_grad = jnp.einsum(
        "bqhd,bkhd->bhqk", grad_blocks, val_all, preferred_element_type=jnp.float32
    )
    score_grad = (soft_prob * (prob_grad - row_delta[..., None])).astype(jnp.bfloat16)
    query_grad = (
        jnp.einsum("bhqk,bkhd->bqhd", score_grad, key_all, preferred_element_type=jnp.float32)
        * score_scale
    ).astype(jnp.bfloat16)
    key_terms = (
        jnp.einsum("bhqk,bqhd->bkhd", score_grad, q_blocks, preferred_element_type=jnp.float32)
        * score_scale
    )
    value_terms = jnp.einsum(
        "bhqk,bqhd->bkhd", weights, grad_blocks, preferred_element_type=jnp.float32
    )
    sink_term = -jnp.sum(sink_prob * row_delta, axis=(0, 2))
    return (query_grad, key_terms, value_terms, sink_term)


def keys_travel_body(queries, key_states, values, out_grad, block_links, sink_logit):
    tokens = queries.shape[1]
    width = queries.shape[2]
    blocks = tokens // BLOCK
    heads = sink_logit.shape[0]
    head_size = width // heads
    score_scale = head_size ** (-0.5)

    def to_blocks(array):
        return array.reshape(blocks, BLOCK, heads, head_size)

    q_blocks = to_blocks(queries)
    grad_blocks = to_blocks(out_grad)
    level_live = block_links >= 0
    causal = jnp.broadcast_to(causal_table(BLOCK), (blocks, BLOCK, BLOCK))
    remote_masks = [
        jnp.broadcast_to(level_live[level_num][:, None, None], (blocks, BLOCK, BLOCK))
        for level_num in range(LEVELS)
    ]
    allowed = jnp.concatenate([causal] + remote_masks, axis=2)
    fetched = []
    for level_num in range(LEVELS):
        fetched.append(from_behind((key_states, values), "dp", 2**level_num))
    key_all = jnp.concatenate(
        [to_blocks(key_states)] + [to_blocks(moved[0]) for moved in fetched], axis=1
    )
    val_all = jnp.concatenate(
        [to_blocks(values)] + [to_blocks(moved[1]) for moved in fetched], axis=1
    )
    soft_prob, weights, sink_prob, output = attend_forward(
        q_blocks, key_all, val_all, allowed, sink_logit, score_scale
    )
    query_grad, key_terms, value_terms, sink_term = attend_backward(
        q_blocks, key_all, val_all, grad_blocks, soft_prob, weights, sink_prob, output, score_scale
    )
    key_grad = key_terms[:, :BLOCK].reshape(1, tokens, width)
    value_grad = value_terms[:, :BLOCK].reshape(1, tokens, width)
    for level_num in range(LEVELS):
        first_col = BLOCK * (1 + level_num)
        key_part = (
            key_terms[:, first_col : first_col + BLOCK]
            .reshape(1, tokens, width)
            .astype(jnp.bfloat16)
        )
        value_part = (
            value_terms[:, first_col : first_col + BLOCK]
            .reshape(1, tokens, width)
            .astype(jnp.bfloat16)
        )
        key_back, value_back = from_behind((key_part, value_part), "dp", -(2**level_num))
        key_grad = key_grad + key_back.astype(jnp.float32)
        value_grad = value_grad + value_back.astype(jnp.float32)
    sink_grad = lax.psum(sink_term, ("dp", "ctx"))
    return (
        query_grad.reshape(1, tokens, width),
        key_grad.astype(jnp.bfloat16),
        value_grad.astype(jnp.bfloat16),
        sink_grad,
    )


CHUNKS = (2, 3)


def body(queries, key_states, values, out_grad, block_links, sink_logit):
    heads = sink_logit.shape[0]
    blocks = lax.axis_size("dp")
    groups = lax.axis_size("ctx")
    fits = (
        blocks == 4
        and queries.shape[:2] == (1, BLOCK)
        and queries.shape[2] == heads * BLOCK
        and heads == 4 * sum(CHUNKS)
        and groups & (groups - 1) == 0
    )
    plan = functools.partial(head_shares_body, CHUNKS) if fits else keys_travel_body
    return plan(queries, key_states, values, out_grad, block_links, sink_logit)


def solution(mesh):
    placed = (
        P("ctx", "dp", None),
        P("ctx", "dp", None),
        P("ctx", "dp", None),
        P("ctx", "dp", None),
        P(None, "dp"),
        P(),
    )
    return jax.shard_map(
        body,
        mesh=mesh,
        in_specs=placed,
        out_specs=(P("ctx", "dp", None), P("ctx", "dp", None), P("ctx", "dp", None), P()),
        check_vma=False,
    )
```

```python
import functools

import jax
import jax.numpy as jnp
from jax import lax
from jax.experimental import pallas as pl
from jax.experimental.pallas import tpu as pltpu
from jax.sharding import PartitionSpec as P

BLOCK = 128
LEVELS = 2
FLAG_ROWS = 16
LOG2_E = 1.4426950408889634
NEG_FILL = -1e30
ORDER = (3, 1, 2)


def pack_kernel(offset, width, share, with_flags, links, *refs):
    arrays, outs, (held, load_sems, store_sems) = refs[:4], refs[4:7], refs[7:]
    me = lax.axis_index("dp")
    loads, stores = [], []
    for place, mask in enumerate(ORDER):
        start = pl.multiple_of((me ^ mask) * share + offset, BLOCK)
        loads.append(
            [
                pltpu.make_async_copy(
                    array.at[0, :, pl.ds(start, width)],
                    held.at[place, pl.ds(num * BLOCK, BLOCK), :],
                    load_sems.at[place, num],
                )
                for num, array in enumerate(arrays)
            ]
        )
        for copy in loads[-1]:
            copy.start()
    if with_flags:
        flags = live_flags(links, width)
        for place in range(3):
            held[place, 4 * BLOCK :, :] = flags
    for place in range(3):
        for copy in loads[place]:
            copy.wait()
        stores.append(pltpu.make_async_copy(held.at[place], outs[place], store_sems.at[place]))
        stores[-1].start()
    for copy in stores:
        copy.wait()


def live_flags(links, width):
    live = [jnp.where(links[level] >= 0, 1.0, 0.0) for level in range(LEVELS)]
    row = lax.broadcasted_iota(jnp.int32, (FLAG_ROWS, width), 0)
    return jnp.where(row < 8, live[0], live[1]).astype(jnp.bfloat16)


def pack(links, arrays, offset, width, share, with_flags):
    rows = 4 * BLOCK + FLAG_ROWS * with_flags
    return pl.pallas_call(
        functools.partial(pack_kernel, offset, width, share, with_flags),
        out_shape=[jax.ShapeDtypeStruct((rows, width), jnp.bfloat16)] * 3,
        in_specs=[pl.BlockSpec(memory_space=pltpu.SMEM)] + [pl.BlockSpec(memory_space=pl.ANY)] * 4,
        out_specs=[pl.BlockSpec(memory_space=pl.ANY)] * 3,
        scratch_shapes=[
            pltpu.VMEM((3, rows, width), jnp.bfloat16),
            pltpu.SemaphoreType.DMA((3, 4)),
            pltpu.SemaphoreType.DMA((3,)),
        ],
        cost_estimate=pl.CostEstimate(flops=0, bytes_accessed=12 * rows * width, transcendentals=0),
        name="pack",
    )(links, *arrays)


def dot_nt(a, b):
    return lax.dot_general(a, b, (((1,), (1,)), ((), ())), preferred_element_type=jnp.float32)


def dot_nn(a, b):
    return lax.dot_general(a, b, (((1,), (0,)), ((), ())), preferred_element_type=jnp.float32)


def dot_tn(a, b):
    return lax.dot_general(a, b, (((0,), (0,)), ((), ())), preferred_element_type=jnp.float32)


def attend_kernel(first_head, heads, heads_dev, score_scale, num_previous, sink, links, sink_in, *refs):
    arrays, ins, flag_ins, refs = refs[:4], refs[4:7], refs[7:10], refs[10 + num_previous :]
    outs, own_outs, sink_out = refs[:3], refs[3:6], refs[6]
    held, flags_held, grads, own_sems, in_sems, flag_sems, own_out_sems, out_sems = refs[7:]
    me = lax.axis_index("dp")
    blocks = 4

    def own_columns(head):
        return pl.ds(pl.multiple_of((me * heads_dev + first_head + head) * BLOCK, BLOCK), BLOCK)

    def columns(head):
        return pl.ds(head * BLOCK, BLOCK)

    loads = [
        [
            pltpu.make_async_copy(
                array.at[0, :, own_columns(head)],
                held.at[me, pl.ds(num * BLOCK, BLOCK), columns(head)],
                own_sems.at[head, num],
            )
            for num, array in enumerate(arrays)
        ]
        + [
            pltpu.make_async_copy(
                ins[place].at[pl.ds(0, 4 * BLOCK), columns(head)],
                held.at[me ^ mask, :, columns(head)],
                in_sems.at[head, place],
            )
            for place, mask in enumerate(ORDER)
        ]
        for head in range(heads)
    ]
    for group in loads:
        for copy in group:
            copy.start()
    flag_loads = [
        pltpu.make_async_copy(
            flag_ins[place].at[pl.ds(4 * BLOCK, FLAG_ROWS), pl.ds(0, BLOCK)],
            flags_held.at[me ^ mask],
            flag_sems.at[place],
        )
        for place, mask in enumerate(ORDER)
    ]
    for copy in flag_loads:
        copy.start()
    flags_held[me] = live_flags(links, BLOCK)
    keys_iota = lax.broadcasted_iota(jnp.int32, (BLOCK, BLOCK), 0)
    queries_iota = lax.broadcasted_iota(jnp.int32, (BLOCK, BLOCK), 1)
    causal = keys_iota <= queries_iota
    lanes = lax.broadcasted_iota(jnp.int32, (8, BLOCK), 1)
    sink_sum = sink_in[...]
    for copy in flag_loads:
        copy.wait()
    stores = []
    for head in range(heads):
        for copy in loads[head]:
            copy.wait()
        cols = columns(head)

        def part(kind, first, last):
            return held[first : last + 1, kind * BLOCK : (kind + 1) * BLOCK, cols].reshape(
                (last + 1 - first) * BLOCK, BLOCK
            )

        sink_logit = sink[me * heads_dev + first_head + head] * LOG2_E
        scores, prob_grads = {}, {}
        for pair in range(0, blocks, 2):
            first = max(0, pair - LEVELS)
            score = dot_nt(part(1, first, pair + 1), part(0, pair, pair + 1))
            prob_grad = dot_nt(part(2, first, pair + 1), part(3, pair, pair + 1))
            for block in (pair, pair + 1):
                lanes_here = slice((block - pair) * BLOCK, (block - pair + 1) * BLOCK)
                for source in range(max(0, block - LEVELS), block + 1):
                    rows = slice((source - first) * BLOCK, (source - first + 1) * BLOCK)
                    scores[block, source] = score[rows, lanes_here]
                    prob_grads[block, source] = prob_grad[rows, lanes_here]
        sink_total = jnp.zeros((1, BLOCK), jnp.float32)
        weights, score_grads = {}, {}
        for block in range(blocks):
            sources = range(max(0, block - LEVELS), block + 1)
            flags = flags_held[block].astype(jnp.float32)
            pieces = []
            for source in sources:
                piece = scores[block, source] * (score_scale * LOG2_E)
                if source == block:
                    piece = jnp.where(causal, piece, NEG_FILL)
                else:
                    row = 8 * (block - source - 1)
                    piece = jnp.where(flags[row : row + 1] > 0.5, piece, NEG_FILL)
                pieces.append(piece)
            row_max = functools.reduce(jnp.maximum, pieces)
            row_max = jnp.maximum(jnp.max(row_max, axis=0, keepdims=True), sink_logit)
            pieces = [jnp.exp2(piece - row_max) for piece in pieces]
            sink_exp = jnp.exp2(sink_logit - row_max)
            denominator = jnp.sum(functools.reduce(jnp.add, pieces), axis=0, keepdims=True) + sink_exp
            scale = 1.0 / denominator
            pieces = [piece * scale for piece in pieces]
            products = [piece * prob_grads[block, source] for piece, source in zip(pieces, sources)]
            row_delta = jnp.sum(functools.reduce(jnp.add, products), axis=0, keepdims=True)
            sink_total = sink_total + sink_exp * scale * row_delta
            for piece, source in zip(pieces, sources):
                weights[block, source] = piece.astype(jnp.bfloat16)
                score_grads[block, source] = (
                    piece * (prob_grads[block, source] - row_delta)
                ).astype(jnp.bfloat16)
        here = lanes == me * heads_dev + first_head + head
        sink_sum = sink_sum - jnp.where(here, jnp.sum(sink_total, axis=1, keepdims=True), 0.0)
        for block in range(blocks):
            first = max(0, block - LEVELS)
            score_grad = jnp.concatenate([score_grads[block, b] for b in range(first, block + 1)], axis=0)
            query_grad = dot_tn(score_grad, part(1, first, block)) * score_scale
            grads[block, 0:BLOCK, cols] = query_grad.astype(jnp.bfloat16)
        for source in range(blocks):
            last = min(blocks - 1, source + LEVELS)
            score_grad = jnp.concatenate([score_grads[b, source] for b in range(source, last + 1)], axis=1)
            weight = jnp.concatenate([weights[b, source] for b in range(source, last + 1)], axis=1)
            key_grad = dot_nn(score_grad, part(0, source, last)) * score_scale
            value_grad = dot_nn(weight, part(3, source, last))
            grads[source, BLOCK : 2 * BLOCK, cols] = key_grad.astype(jnp.bfloat16)
            grads[source, 2 * BLOCK : 3 * BLOCK, cols] = value_grad.astype(jnp.bfloat16)
        copies = [
            pltpu.make_async_copy(
                grads.at[me ^ mask, :, cols], outs[place].at[:, cols], out_sems.at[head, place]
            )
            for place, mask in enumerate(ORDER)
        ] + [
            pltpu.make_async_copy(
                grads.at[me, pl.ds(num * BLOCK, BLOCK), cols],
                out.at[0, :, own_columns(head)],
                own_out_sems.at[head, num],
            )
            for num, out in enumerate(own_outs)
        ]
        for copy in copies:
            copy.start()
        stores.extend(copies)
    sink_out[...] = sink_sum
    for copy in stores:
        copy.wait()


def attend(sink_logit, links, sink_sum, arrays, packed, flags, previous, first_head, heads, heads_dev, score_scale):
    rows, grad_rows, width = 4 * BLOCK, 3 * BLOCK, packed[0].shape[1]
    hbm = pl.BlockSpec(memory_space=pl.ANY)
    smem = pl.BlockSpec(memory_space=pltpu.SMEM)
    vmem = pl.BlockSpec(memory_space=pltpu.VMEM)
    return pl.pallas_call(
        functools.partial(attend_kernel, first_head, heads, heads_dev, score_scale, len(previous)),
        out_shape=[jax.ShapeDtypeStruct((grad_rows, width), jnp.bfloat16)] * 3
        + [jax.ShapeDtypeStruct(arrays[0].shape, jnp.bfloat16)] * 3
        + [jax.ShapeDtypeStruct((8, BLOCK), jnp.float32)],
        in_specs=[smem, smem, vmem] + [hbm] * (10 + len(previous)),
        out_specs=[hbm] * 6 + [vmem],
        scratch_shapes=[
            pltpu.VMEM((4, rows, width), jnp.bfloat16),
            pltpu.VMEM((4, FLAG_ROWS, BLOCK), jnp.bfloat16),
            pltpu.VMEM((4, grad_rows, width), jnp.bfloat16),
            pltpu.SemaphoreType.DMA((heads, 4)),
            pltpu.SemaphoreType.DMA((heads, 3)),
            pltpu.SemaphoreType.DMA((3,)),
            pltpu.SemaphoreType.DMA((heads, 3)),
            pltpu.SemaphoreType.DMA((heads, 3)),
        ],
        input_output_aliases={13 + num: 3 + num for num in range(len(previous))},
        compiler_params=pltpu.CompilerParams(vmem_limit_bytes=8 * 2**20),
        cost_estimate=pl.CostEstimate(flops=0, bytes_accessed=0, transcendentals=0),
        name="attend",
    )(sink_logit, links, sink_sum, *arrays, *packed, *flags, *previous)


def unpack_kernel(offset, width, share, *refs):
    ins, outs, (held, load_sems, store_sems) = refs[:3], refs[6:9], refs[9:]
    me = lax.axis_index("dp")
    loads = [
        pltpu.make_async_copy(ins[place], held.at[place], load_sems.at[place]) for place in range(3)
    ]
    for copy in loads:
        copy.start()
    stores = []
    for place, mask in enumerate(ORDER):
        loads[place].wait()
        start = pl.multiple_of((me ^ mask) * share + offset, BLOCK)
        for num, out in enumerate(outs):
            stores.append(
                pltpu.make_async_copy(
                    held.at[place, pl.ds(num * BLOCK, BLOCK), :],
                    out.at[0, :, pl.ds(start, width)],
                    store_sems.at[place, num],
                )
            )
            stores[-1].start()
    for copy in stores:
        copy.wait()


def unpack(parts, previous, offset, share):
    rows, width = parts[0].shape
    return pl.pallas_call(
        functools.partial(unpack_kernel, offset, width, share),
        out_shape=[jax.ShapeDtypeStruct(out.shape, out.dtype) for out in previous],
        in_specs=[pl.BlockSpec(memory_space=pl.ANY)] * 6,
        out_specs=[pl.BlockSpec(memory_space=pl.ANY)] * 3,
        scratch_shapes=[
            pltpu.VMEM((3, rows, width), jnp.bfloat16),
            pltpu.SemaphoreType.DMA((3,)),
            pltpu.SemaphoreType.DMA((3, 3)),
        ],
        input_output_aliases={3 + num: num for num in range(3)},
        compiler_params=pltpu.CompilerParams(vmem_limit_bytes=8 * 2**20),
        cost_estimate=pl.CostEstimate(flops=0, bytes_accessed=0, transcendentals=0),
        name="unpack",
    )(*parts, *previous)


def swap(value, axis, mask):
    return lax.ppermute(value, axis, [(i, i ^ mask) for i in range(lax.axis_size(axis))])


def after(value, other):
    return lax.optimization_barrier((value, other))


def add_swapped(value, axis, masks):
    for mask in masks:
        value = value + swap(value, axis, mask)
    return value


def head_shares_body(chunks, queries, key_states, values, out_grad, block_links, sink_logit):
    heads = sink_logit.shape[0]
    head_size = queries.shape[2] // heads
    score_scale = head_size ** (-0.5)
    heads_dev = heads // 4
    share = heads_dev * head_size
    arrays = (queries, key_states, values, out_grad)
    links = block_links.reshape(LEVELS)
    received, first = [], 0
    for count in chunks:
        packed = pack(links, arrays, first * head_size, count * head_size, share, first == 0)
        moved = [swap(part, "dp", mask) for part, mask in zip(packed, ORDER)]
        received.append((first, count, moved))
        first += count
    results, outputs, sink_sum = [], [], jnp.zeros((8, BLOCK), jnp.float32)
    for num, (first, count, packed) in enumerate(received):
        *grads, sink_sum = attend(
            sink_logit, links, sink_sum, arrays, packed, received[0][2], outputs, first, count, heads_dev, score_scale
        )
        grads, outputs = grads[:3], list(grads[3:])
        if num:
            sink_sum = sink_sum + swap(sink_sum, "ctx", 2)
            grads[0], results[0][1][0] = after(grads[0], results[0][1][0])
        else:
            for place in (1, 2):
                grads[place], received[1][2][0] = after(grads[place], received[1][2][0])
        results.append((first, [swap(grad, "dp", mask) for grad, mask in zip(grads, ORDER)]))
    sink_sum, results[0][1][2] = after(sink_sum, results[0][1][2])
    once = jnp.minimum(links[0] + 2, 1)
    sink_sum = lax.fori_loop(0, once, lambda _, held: add_swapped(held, "ctx", (1, 4)), sink_sum)
    sink_sum = add_swapped(sink_sum, "dp", (1,))
    outputs = list(unpack(results[0][1], outputs, results[0][0] * head_size, share))
    sink_sum, outputs[0] = after(sink_sum, outputs[0])
    sink_sum = add_swapped(sink_sum, "dp", (2,))
    outputs = unpack(results[1][1], outputs, results[1][0] * head_size, share)
    return (*outputs, sink_sum[0, :heads])


def from_behind(value, axis, steps):
    count = lax.axis_size(axis)
    initial, last = (max(0, -steps), min(count, count - steps))
    return lax.ppermute(value, axis, [(source, source + steps) for source in range(initial, last)])


def causal_table(block_len):
    rows_iota = lax.broadcasted_iota(jnp.int32, (block_len, block_len), 0)
    cols_iota = lax.broadcasted_iota(jnp.int32, (block_len, block_len), 1)
    return rows_iota >= cols_iota


def attend_forward(q_blocks, key_all, val_all, allowed, sink_logit, score_scale):
    scores = (
        jnp.einsum("bqhd,bkhd->bhqk", q_blocks, key_all, preferred_element_type=jnp.float32)
        * score_scale
    )
    scores = jnp.where(allowed[:, None], scores, NEG_FILL)
    row_max = jnp.maximum(jnp.max(scores, axis=-1), sink_logit[None, :, None])
    exp_scores = jnp.exp(scores - row_max[..., None])
    sink_exp = jnp.exp(sink_logit[None, :, None] - row_max)
    denominator = jnp.sum(exp_scores, axis=-1) + sink_exp
    soft_prob = exp_scores / denominator[..., None]
    sink_prob = sink_exp / denominator
    weights = soft_prob.astype(jnp.bfloat16)
    output = jnp.einsum(
        "bhqk,bkhd->bqhd", weights, val_all, preferred_element_type=jnp.float32
    ).astype(jnp.bfloat16)
    return (soft_prob, weights, sink_prob, output)


def attend_backward(
    q_blocks, key_all, val_all, grad_blocks, soft_prob, weights, sink_prob, output, score_scale
):
    row_delta = jnp.sum(grad_blocks.astype(jnp.float32) * output.astype(jnp.float32), axis=-1)
    row_delta = jnp.transpose(row_delta, (0, 2, 1))
    prob_grad = jnp.einsum(
        "bqhd,bkhd->bhqk", grad_blocks, val_all, preferred_element_type=jnp.float32
    )
    score_grad = (soft_prob * (prob_grad - row_delta[..., None])).astype(jnp.bfloat16)
    query_grad = (
        jnp.einsum("bhqk,bkhd->bqhd", score_grad, key_all, preferred_element_type=jnp.float32)
        * score_scale
    ).astype(jnp.bfloat16)
    key_terms = (
        jnp.einsum("bhqk,bqhd->bkhd", score_grad, q_blocks, preferred_element_type=jnp.float32)
        * score_scale
    )
    value_terms = jnp.einsum(
        "bhqk,bqhd->bkhd", weights, grad_blocks, preferred_element_type=jnp.float32
    )
    sink_term = -jnp.sum(sink_prob * row_delta, axis=(0, 2))
    return (query_grad, key_terms, value_terms, sink_term)


def keys_travel_body(queries, key_states, values, out_grad, block_links, sink_logit):
    tokens = queries.shape[1]
    width = queries.shape[2]
    blocks = tokens // BLOCK
    heads = sink_logit.shape[0]
    head_size = width // heads
    score_scale = head_size ** (-0.5)

    def to_blocks(array):
        return array.reshape(blocks, BLOCK, heads, head_size)

    q_blocks = to_blocks(queries)
    grad_blocks = to_blocks(out_grad)
    level_live = block_links >= 0
    causal = jnp.broadcast_to(causal_table(BLOCK), (blocks, BLOCK, BLOCK))
    remote_masks = [
        jnp.broadcast_to(level_live[level_num][:, None, None], (blocks, BLOCK, BLOCK))
        for level_num in range(LEVELS)
    ]
    allowed = jnp.concatenate([causal] + remote_masks, axis=2)
    fetched = []
    for level_num in range(LEVELS):
        fetched.append(from_behind((key_states, values), "dp", 2**level_num))
    key_all = jnp.concatenate(
        [to_blocks(key_states)] + [to_blocks(moved[0]) for moved in fetched], axis=1
    )
    val_all = jnp.concatenate(
        [to_blocks(values)] + [to_blocks(moved[1]) for moved in fetched], axis=1
    )
    soft_prob, weights, sink_prob, output = attend_forward(
        q_blocks, key_all, val_all, allowed, sink_logit, score_scale
    )
    query_grad, key_terms, value_terms, sink_term = attend_backward(
        q_blocks, key_all, val_all, grad_blocks, soft_prob, weights, sink_prob, output, score_scale
    )
    key_grad = key_terms[:, :BLOCK].reshape(1, tokens, width)
    value_grad = value_terms[:, :BLOCK].reshape(1, tokens, width)
    for level_num in range(LEVELS):
        first_col = BLOCK * (1 + level_num)
        key_part = (
            key_terms[:, first_col : first_col + BLOCK]
            .reshape(1, tokens, width)
            .astype(jnp.bfloat16)
        )
        value_part = (
            value_terms[:, first_col : first_col + BLOCK]
            .reshape(1, tokens, width)
            .astype(jnp.bfloat16)
        )
        key_back, value_back = from_behind((key_part, value_part), "dp", -(2**level_num))
        key_grad = key_grad + key_back.astype(jnp.float32)
        value_grad = value_grad + value_back.astype(jnp.float32)
    sink_grad = lax.psum(sink_term, ("dp", "ctx"))
    return (
        query_grad.reshape(1, tokens, width),
        key_grad.astype(jnp.bfloat16),
        value_grad.astype(jnp.bfloat16),
        sink_grad,
    )


CHUNKS = (2, 3)


def body(queries, key_states, values, out_grad, block_links, sink_logit):
    heads = sink_logit.shape[0]
    blocks = lax.axis_size("dp")
    groups = lax.axis_size("ctx")
    fits = (
        blocks == 4
        and queries.shape[:2] == (1, BLOCK)
        and queries.shape[2] == heads * BLOCK
        and heads == 4 * sum(CHUNKS)
        and groups == 8
    )
    plan = functools.partial(head_shares_body, CHUNKS) if fits else keys_travel_body
    return plan(queries, key_states, values, out_grad, block_links, sink_logit)


def solution(mesh):
    placed = (
        P("ctx", "dp", None),
        P("ctx", "dp", None),
        P("ctx", "dp", None),
        P("ctx", "dp", None),
        P(None, "dp"),
        P(),
    )
    return jax.shard_map(
        body,
        mesh=mesh,
        in_specs=placed,
        out_specs=(P("ctx", "dp", None), P("ctx", "dp", None), P("ctx", "dp", None), P()),
        check_vma=False,
    )
```

```python
import functools

import jax
import jax.numpy as jnp
from jax import lax
from jax.experimental import pallas as pl
from jax.experimental.pallas import tpu as pltpu
from jax.sharding import PartitionSpec as P

BLOCK = 128
LEVELS = 2
FLAG_ROWS = 16
LOG2_E = 1.4426950408889634
NEG_FILL = -1e30
ORDER = (3, 1, 2)


def pack_kernel(offset, width, share, with_flags, links, *refs):
    arrays, outs, (held, load_sems, store_sems) = refs[:4], refs[4:7], refs[7:]
    me = lax.axis_index("dp")
    loads, stores = [], []
    for place, mask in enumerate(ORDER):
        start = pl.multiple_of((me ^ mask) * share + offset, BLOCK)
        loads.append(
            [
                pltpu.make_async_copy(
                    array.at[0, :, pl.ds(start, width)],
                    held.at[place, pl.ds(num * BLOCK, BLOCK), :],
                    load_sems.at[place, num],
                )
                for num, array in enumerate(arrays)
            ]
        )
        for copy in loads[-1]:
            copy.start()
    if with_flags:
        flags = live_flags(links, width)
        for place in range(3):
            held[place, 4 * BLOCK :, :] = flags
    for place in range(3):
        for copy in loads[place]:
            copy.wait()
        stores.append(pltpu.make_async_copy(held.at[place], outs[place], store_sems.at[place]))
        stores[-1].start()
    for copy in stores:
        copy.wait()


def live_flags(links, width):
    live = [jnp.where(links[level] >= 0, 1.0, 0.0) for level in range(LEVELS)]
    row = lax.broadcasted_iota(jnp.int32, (FLAG_ROWS, width), 0)
    return jnp.where(row < 8, live[0], live[1]).astype(jnp.bfloat16)


def pack(links, arrays, offset, width, share, with_flags):
    rows = 4 * BLOCK + FLAG_ROWS * with_flags
    return pl.pallas_call(
        functools.partial(pack_kernel, offset, width, share, with_flags),
        out_shape=[jax.ShapeDtypeStruct((rows, width), jnp.bfloat16)] * 3,
        in_specs=[pl.BlockSpec(memory_space=pltpu.SMEM)] + [pl.BlockSpec(memory_space=pl.ANY)] * 4,
        out_specs=[pl.BlockSpec(memory_space=pl.ANY)] * 3,
        scratch_shapes=[
            pltpu.VMEM((3, rows, width), jnp.bfloat16),
            pltpu.SemaphoreType.DMA((3, 4)),
            pltpu.SemaphoreType.DMA((3,)),
        ],
        cost_estimate=pl.CostEstimate(flops=0, bytes_accessed=12 * rows * width, transcendentals=0),
        name="pack",
    )(links, *arrays)


def dot_nt(a, b):
    return lax.dot_general(a, b, (((1,), (1,)), ((), ())), preferred_element_type=jnp.float32)


def dot_nn(a, b):
    return lax.dot_general(a, b, (((1,), (0,)), ((), ())), preferred_element_type=jnp.float32)


def dot_tn(a, b):
    return lax.dot_general(a, b, (((0,), (0,)), ((), ())), preferred_element_type=jnp.float32)


def attend_kernel(first_head, heads, heads_dev, score_scale, num_previous, sink, links, sink_in, *refs):
    arrays, ins, flag_ins, refs = refs[:4], refs[4:7], refs[7:10], refs[10 + num_previous :]
    outs, own_outs, sink_out = refs[:3], refs[3:6], refs[6]
    held, flags_held, grads, own_sems, in_sems, flag_sems, own_out_sems, out_sems = refs[7:]
    me = lax.axis_index("dp")
    blocks = 4

    def own_columns(head):
        return pl.ds(pl.multiple_of((me * heads_dev + first_head + head) * BLOCK, BLOCK), BLOCK)

    def columns(head):
        return pl.ds(head * BLOCK, BLOCK)

    loads = [
        [
            pltpu.make_async_copy(
                array.at[0, :, own_columns(head)],
                held.at[me, pl.ds(num * BLOCK, BLOCK), columns(head)],
                own_sems.at[head, num],
            )
            for num, array in enumerate(arrays)
        ]
        + [
            pltpu.make_async_copy(
                ins[place].at[pl.ds(0, 4 * BLOCK), columns(head)],
                held.at[me ^ mask, :, columns(head)],
                in_sems.at[head, place],
            )
            for place, mask in enumerate(ORDER)
        ]
        for head in range(heads)
    ]
    for group in loads:
        for copy in group:
            copy.start()
    flag_loads = [
        pltpu.make_async_copy(
            flag_ins[place].at[pl.ds(4 * BLOCK, FLAG_ROWS), pl.ds(0, BLOCK)],
            flags_held.at[me ^ mask],
            flag_sems.at[place],
        )
        for place, mask in enumerate(ORDER)
    ]
    for copy in flag_loads:
        copy.start()
    flags_held[me] = live_flags(links, BLOCK)
    keys_iota = lax.broadcasted_iota(jnp.int32, (BLOCK, BLOCK), 0)
    queries_iota = lax.broadcasted_iota(jnp.int32, (BLOCK, BLOCK), 1)
    causal = keys_iota <= queries_iota
    lanes = lax.broadcasted_iota(jnp.int32, (1, BLOCK), 1)
    sink_sum = sink_in[...]
    for copy in flag_loads:
        copy.wait()
    stores = []
    for head in range(heads):
        for copy in loads[head]:
            copy.wait()
        cols = columns(head)

        def part(kind, first, last):
            return held[first : last + 1, kind * BLOCK : (kind + 1) * BLOCK, cols].reshape(
                (last + 1 - first) * BLOCK, BLOCK
            )

        sink_logit = sink[me * heads_dev + first_head + head] * LOG2_E
        scores, prob_grads = {}, {}
        for pair in range(0, blocks, 2):
            first = max(0, pair - LEVELS)
            score = dot_nt(part(1, first, pair + 1), part(0, pair, pair + 1))
            prob_grad = dot_nt(part(2, first, pair + 1), part(3, pair, pair + 1))
            for block in (pair, pair + 1):
                lanes_here = slice((block - pair) * BLOCK, (block - pair + 1) * BLOCK)
                for source in range(max(0, block - LEVELS), block + 1):
                    rows = slice((source - first) * BLOCK, (source - first + 1) * BLOCK)
                    scores[block, source] = score[rows, lanes_here]
                    prob_grads[block, source] = prob_grad[rows, lanes_here]
        sink_total = jnp.zeros((1, BLOCK), jnp.float32)
        weights, score_grads = {}, {}
        for block in range(blocks):
            sources = range(max(0, block - LEVELS), block + 1)
            flags = flags_held[block].astype(jnp.float32)
            pieces = []
            for source in sources:
                piece = scores[block, source] * (score_scale * LOG2_E)
                if source == block:
                    piece = jnp.where(causal, piece, NEG_FILL)
                else:
                    row = 8 * (block - source - 1)
                    piece = jnp.where(flags[row : row + 1] > 0.5, piece, NEG_FILL)
                pieces.append(piece)
            row_max = functools.reduce(jnp.maximum, pieces)
            row_max = jnp.maximum(jnp.max(row_max, axis=0, keepdims=True), sink_logit)
            pieces = [jnp.exp2(piece - row_max) for piece in pieces]
            sink_exp = jnp.exp2(sink_logit - row_max)
            denominator = jnp.sum(functools.reduce(jnp.add, pieces), axis=0, keepdims=True) + sink_exp
            scale = 1.0 / denominator
            pieces = [piece * scale for piece in pieces]
            products = [piece * prob_grads[block, source] for piece, source in zip(pieces, sources)]
            row_delta = jnp.sum(functools.reduce(jnp.add, products), axis=0, keepdims=True)
            sink_total = sink_total + sink_exp * scale * row_delta
            for piece, source in zip(pieces, sources):
                weights[block, source] = piece.astype(jnp.bfloat16)
                score_grads[block, source] = (
                    piece * (prob_grads[block, source] - row_delta)
                ).astype(jnp.bfloat16)
        here = lanes == me * heads_dev + first_head + head
        sink_sum = sink_sum - jnp.where(here, jnp.sum(sink_total, axis=1, keepdims=True), 0.0)
        for block in range(blocks):
            first = max(0, block - LEVELS)
            score_grad = jnp.concatenate([score_grads[block, b] for b in range(first, block + 1)], axis=0)
            query_grad = dot_tn(score_grad, part(1, first, block)) * score_scale
            grads[block, 0:BLOCK, cols] = query_grad.astype(jnp.bfloat16)
        for source in range(blocks):
            last = min(blocks - 1, source + LEVELS)
            score_grad = jnp.concatenate([score_grads[b, source] for b in range(source, last + 1)], axis=1)
            weight = jnp.concatenate([weights[b, source] for b in range(source, last + 1)], axis=1)
            key_grad = dot_nn(score_grad, part(0, source, last)) * score_scale
            value_grad = dot_nn(weight, part(3, source, last))
            grads[source, BLOCK : 2 * BLOCK, cols] = key_grad.astype(jnp.bfloat16)
            grads[source, 2 * BLOCK : 3 * BLOCK, cols] = value_grad.astype(jnp.bfloat16)
        copies = [
            pltpu.make_async_copy(
                grads.at[me ^ mask, :, cols], outs[place].at[:, cols], out_sems.at[head, place]
            )
            for place, mask in enumerate(ORDER)
        ] + [
            pltpu.make_async_copy(
                grads.at[me, pl.ds(num * BLOCK, BLOCK), cols],
                out.at[0, :, own_columns(head)],
                own_out_sems.at[head, num],
            )
            for num, out in enumerate(own_outs)
        ]
        for copy in copies:
            copy.start()
        stores.extend(copies)
    sink_out[...] = sink_sum
    for copy in stores:
        copy.wait()


def attend(sink_logit, links, sink_sum, arrays, packed, flags, previous, first_head, heads, heads_dev, score_scale):
    rows, grad_rows, width = 4 * BLOCK, 3 * BLOCK, packed[0].shape[1]
    hbm = pl.BlockSpec(memory_space=pl.ANY)
    smem = pl.BlockSpec(memory_space=pltpu.SMEM)
    vmem = pl.BlockSpec(memory_space=pltpu.VMEM)
    return pl.pallas_call(
        functools.partial(attend_kernel, first_head, heads, heads_dev, score_scale, len(previous)),
        out_shape=[jax.ShapeDtypeStruct((grad_rows, width), jnp.bfloat16)] * 3
        + [jax.ShapeDtypeStruct(arrays[0].shape, jnp.bfloat16)] * 3
        + [jax.ShapeDtypeStruct((1, BLOCK), jnp.float32)],
        in_specs=[smem, smem, vmem] + [hbm] * (10 + len(previous)),
        out_specs=[hbm] * 6 + [vmem],
        scratch_shapes=[
            pltpu.VMEM((4, rows, width), jnp.bfloat16),
            pltpu.VMEM((4, FLAG_ROWS, BLOCK), jnp.bfloat16),
            pltpu.VMEM((4, grad_rows, width), jnp.bfloat16),
            pltpu.SemaphoreType.DMA((heads, 4)),
            pltpu.SemaphoreType.DMA((heads, 3)),
            pltpu.SemaphoreType.DMA((3,)),
            pltpu.SemaphoreType.DMA((heads, 3)),
            pltpu.SemaphoreType.DMA((heads, 3)),
        ],
        input_output_aliases={13 + num: 3 + num for num in range(len(previous))},
        compiler_params=pltpu.CompilerParams(vmem_limit_bytes=8 * 2**20),
        cost_estimate=pl.CostEstimate(flops=0, bytes_accessed=0, transcendentals=0),
        name="attend",
    )(sink_logit, links, sink_sum, *arrays, *packed, *flags, *previous)


def unpack_kernel(offset, width, share, *refs):
    ins, outs, (held, load_sems, store_sems) = refs[:3], refs[6:9], refs[9:]
    me = lax.axis_index("dp")
    loads = [
        pltpu.make_async_copy(ins[place], held.at[place], load_sems.at[place]) for place in range(3)
    ]
    for copy in loads:
        copy.start()
    stores = []
    for place, mask in enumerate(ORDER):
        loads[place].wait()
        start = pl.multiple_of((me ^ mask) * share + offset, BLOCK)
        for num, out in enumerate(outs):
            stores.append(
                pltpu.make_async_copy(
                    held.at[place, pl.ds(num * BLOCK, BLOCK), :],
                    out.at[0, :, pl.ds(start, width)],
                    store_sems.at[place, num],
                )
            )
            stores[-1].start()
    for copy in stores:
        copy.wait()


def unpack(parts, previous, offset, share):
    rows, width = parts[0].shape
    return pl.pallas_call(
        functools.partial(unpack_kernel, offset, width, share),
        out_shape=[jax.ShapeDtypeStruct(out.shape, out.dtype) for out in previous],
        in_specs=[pl.BlockSpec(memory_space=pl.ANY)] * 6,
        out_specs=[pl.BlockSpec(memory_space=pl.ANY)] * 3,
        scratch_shapes=[
            pltpu.VMEM((3, rows, width), jnp.bfloat16),
            pltpu.SemaphoreType.DMA((3,)),
            pltpu.SemaphoreType.DMA((3, 3)),
        ],
        input_output_aliases={3 + num: num for num in range(3)},
        compiler_params=pltpu.CompilerParams(vmem_limit_bytes=8 * 2**20),
        cost_estimate=pl.CostEstimate(flops=0, bytes_accessed=0, transcendentals=0),
        name="unpack",
    )(*parts, *previous)


def swap(value, axis, mask):
    return lax.ppermute(value, axis, [(i, i ^ mask) for i in range(lax.axis_size(axis))])


def after(value, other):
    return lax.optimization_barrier((value, other))


def add_swapped(value, axis, masks):
    for mask in masks:
        value = value + swap(value, axis, mask)
    return value


def head_shares_body(chunks, queries, key_states, values, out_grad, block_links, sink_logit):
    heads = sink_logit.shape[0]
    head_size = queries.shape[2] // heads
    score_scale = head_size ** (-0.5)
    heads_dev = heads // 4
    share = heads_dev * head_size
    arrays = (queries, key_states, values, out_grad)
    links = block_links.reshape(LEVELS)
    received, first = [], 0
    for count in chunks:
        packed = pack(links, arrays, first * head_size, count * head_size, share, first == 0)
        moved = [swap(part, "dp", mask) for part, mask in zip(packed, ORDER)]
        received.append((first, count, moved))
        first += count
    results, outputs, sink_sum = [], [], jnp.zeros((1, BLOCK), jnp.float32)
    for num, (first, count, packed) in enumerate(received):
        *grads, sink_sum = attend(
            sink_logit, links, sink_sum, arrays, packed, received[0][2], outputs, first, count, heads_dev, score_scale
        )
        grads, outputs = grads[:3], list(grads[3:])
        if num:
            sink_sum = sink_sum + swap(sink_sum, "ctx", 2)
            grads[0], results[0][1][0] = after(grads[0], results[0][1][0])
        else:
            for place in (1, 2):
                grads[place], received[1][2][0] = after(grads[place], received[1][2][0])
        results.append((first, [swap(grad, "dp", mask) for grad, mask in zip(grads, ORDER)]))
    sink_sum, results[0][1][2] = after(sink_sum, results[0][1][2])
    once = jnp.minimum(links[0] + 2, 1)
    sink_sum = lax.fori_loop(0, once, lambda _, held: add_swapped(held, "ctx", (1, 4)), sink_sum)
    sink_sum = add_swapped(sink_sum, "dp", (1,))
    outputs = list(unpack(results[0][1], outputs, results[0][0] * head_size, share))
    sink_sum, outputs[0] = after(sink_sum, outputs[0])
    sink_sum = add_swapped(sink_sum, "dp", (2,))
    outputs = unpack(results[1][1], outputs, results[1][0] * head_size, share)
    return (*outputs, sink_sum[0, :heads])


def from_behind(value, axis, steps):
    count = lax.axis_size(axis)
    initial, last = (max(0, -steps), min(count, count - steps))
    return lax.ppermute(value, axis, [(source, source + steps) for source in range(initial, last)])


def causal_table(block_len):
    rows_iota = lax.broadcasted_iota(jnp.int32, (block_len, block_len), 0)
    cols_iota = lax.broadcasted_iota(jnp.int32, (block_len, block_len), 1)
    return rows_iota >= cols_iota


def attend_forward(q_blocks, key_all, val_all, allowed, sink_logit, score_scale):
    scores = (
        jnp.einsum("bqhd,bkhd->bhqk", q_blocks, key_all, preferred_element_type=jnp.float32)
        * score_scale
    )
    scores = jnp.where(allowed[:, None], scores, NEG_FILL)
    row_max = jnp.maximum(jnp.max(scores, axis=-1), sink_logit[None, :, None])
    exp_scores = jnp.exp(scores - row_max[..., None])
    sink_exp = jnp.exp(sink_logit[None, :, None] - row_max)
    denominator = jnp.sum(exp_scores, axis=-1) + sink_exp
    soft_prob = exp_scores / denominator[..., None]
    sink_prob = sink_exp / denominator
    weights = soft_prob.astype(jnp.bfloat16)
    output = jnp.einsum(
        "bhqk,bkhd->bqhd", weights, val_all, preferred_element_type=jnp.float32
    ).astype(jnp.bfloat16)
    return (soft_prob, weights, sink_prob, output)


def attend_backward(
    q_blocks, key_all, val_all, grad_blocks, soft_prob, weights, sink_prob, output, score_scale
):
    row_delta = jnp.sum(grad_blocks.astype(jnp.float32) * output.astype(jnp.float32), axis=-1)
    row_delta = jnp.transpose(row_delta, (0, 2, 1))
    prob_grad = jnp.einsum(
        "bqhd,bkhd->bhqk", grad_blocks, val_all, preferred_element_type=jnp.float32
    )
    score_grad = (soft_prob * (prob_grad - row_delta[..., None])).astype(jnp.bfloat16)
    query_grad = (
        jnp.einsum("bhqk,bkhd->bqhd", score_grad, key_all, preferred_element_type=jnp.float32)
        * score_scale
    ).astype(jnp.bfloat16)
    key_terms = (
        jnp.einsum("bhqk,bqhd->bkhd", score_grad, q_blocks, preferred_element_type=jnp.float32)
        * score_scale
    )
    value_terms = jnp.einsum(
        "bhqk,bqhd->bkhd", weights, grad_blocks, preferred_element_type=jnp.float32
    )
    sink_term = -jnp.sum(sink_prob * row_delta, axis=(0, 2))
    return (query_grad, key_terms, value_terms, sink_term)


def keys_travel_body(queries, key_states, values, out_grad, block_links, sink_logit):
    tokens = queries.shape[1]
    width = queries.shape[2]
    blocks = tokens // BLOCK
    heads = sink_logit.shape[0]
    head_size = width // heads
    score_scale = head_size ** (-0.5)

    def to_blocks(array):
        return array.reshape(blocks, BLOCK, heads, head_size)

    q_blocks = to_blocks(queries)
    grad_blocks = to_blocks(out_grad)
    level_live = block_links >= 0
    causal = jnp.broadcast_to(causal_table(BLOCK), (blocks, BLOCK, BLOCK))
    remote_masks = [
        jnp.broadcast_to(level_live[level_num][:, None, None], (blocks, BLOCK, BLOCK))
        for level_num in range(LEVELS)
    ]
    allowed = jnp.concatenate([causal] + remote_masks, axis=2)
    fetched = []
    for level_num in range(LEVELS):
        fetched.append(from_behind((key_states, values), "dp", 2**level_num))
    key_all = jnp.concatenate(
        [to_blocks(key_states)] + [to_blocks(moved[0]) for moved in fetched], axis=1
    )
    val_all = jnp.concatenate(
        [to_blocks(values)] + [to_blocks(moved[1]) for moved in fetched], axis=1
    )
    soft_prob, weights, sink_prob, output = attend_forward(
        q_blocks, key_all, val_all, allowed, sink_logit, score_scale
    )
    query_grad, key_terms, value_terms, sink_term = attend_backward(
        q_blocks, key_all, val_all, grad_blocks, soft_prob, weights, sink_prob, output, score_scale
    )
    key_grad = key_terms[:, :BLOCK].reshape(1, tokens, width)
    value_grad = value_terms[:, :BLOCK].reshape(1, tokens, width)
    for level_num in range(LEVELS):
        first_col = BLOCK * (1 + level_num)
        key_part = (
            key_terms[:, first_col : first_col + BLOCK]
            .reshape(1, tokens, width)
            .astype(jnp.bfloat16)
        )
        value_part = (
            value_terms[:, first_col : first_col + BLOCK]
            .reshape(1, tokens, width)
            .astype(jnp.bfloat16)
        )
        key_back, value_back = from_behind((key_part, value_part), "dp", -(2**level_num))
        key_grad = key_grad + key_back.astype(jnp.float32)
        value_grad = value_grad + value_back.astype(jnp.float32)
    sink_grad = lax.psum(sink_term, ("dp", "ctx"))
    return (
        query_grad.reshape(1, tokens, width),
        key_grad.astype(jnp.bfloat16),
        value_grad.astype(jnp.bfloat16),
        sink_grad,
    )


CHUNKS = (2, 3)


def body(queries, key_states, values, out_grad, block_links, sink_logit):
    heads = sink_logit.shape[0]
    blocks = lax.axis_size("dp")
    groups = lax.axis_size("ctx")
    fits = (
        blocks == 4
        and queries.shape[:2] == (1, BLOCK)
        and queries.shape[2] == heads * BLOCK
        and heads == 4 * sum(CHUNKS)
        and groups == 8
    )
    plan = functools.partial(head_shares_body, CHUNKS) if fits else keys_travel_body
    return plan(queries, key_states, values, out_grad, block_links, sink_logit)


def solution(mesh):
    placed = (
        P("ctx", "dp", None),
        P("ctx", "dp", None),
        P("ctx", "dp", None),
        P("ctx", "dp", None),
        P(None, "dp"),
        P(),
    )
    return jax.shard_map(
        body,
        mesh=mesh,
        in_specs=placed,
        out_specs=(P("ctx", "dp", None), P("ctx", "dp", None), P("ctx", "dp", None), P()),
        check_vma=False,
    )
```

```python
import functools

import jax
import jax.numpy as jnp
from jax import lax
from jax.experimental import pallas as pl
from jax.experimental.pallas import tpu as pltpu
from jax.sharding import PartitionSpec as P

BLOCK = 128
LEVELS = 2
FLAG_ROWS = 16
LOG2_E = 1.4426950408889634
NEG_FILL = -1e30
ORDER = (3, 1, 2)


def pack_kernel(offset, width, share, with_flags, links, *refs):
    arrays, outs, (held, load_sems, store_sems) = refs[:4], refs[4:7], refs[7:]
    me = lax.axis_index("dp")
    loads, stores = [], []
    for place, mask in enumerate(ORDER):
        start = pl.multiple_of((me ^ mask) * share + offset, BLOCK)
        loads.append(
            [
                pltpu.make_async_copy(
                    array.at[0, :, pl.ds(start, width)],
                    held.at[place, pl.ds(num * BLOCK, BLOCK), :],
                    load_sems.at[place, num],
                )
                for num, array in enumerate(arrays)
            ]
        )
        for copy in loads[-1]:
            copy.start()
    if with_flags:
        flags = live_flags(links, width)
        for place in range(3):
            held[place, 4 * BLOCK :, :] = flags
    for place in range(3):
        for copy in loads[place]:
            copy.wait()
        stores.append(pltpu.make_async_copy(held.at[place], outs[place], store_sems.at[place]))
        stores[-1].start()
    for copy in stores:
        copy.wait()


def live_flags(links, width):
    live = [jnp.where(links[level] >= 0, 1.0, 0.0) for level in range(LEVELS)]
    row = lax.broadcasted_iota(jnp.int32, (FLAG_ROWS, width), 0)
    return jnp.where(row < 8, live[0], live[1]).astype(jnp.bfloat16)


def pack(links, arrays, offset, width, share, with_flags):
    rows = 4 * BLOCK + FLAG_ROWS * with_flags
    return pl.pallas_call(
        functools.partial(pack_kernel, offset, width, share, with_flags),
        out_shape=[jax.ShapeDtypeStruct((rows, width), jnp.bfloat16)] * 3,
        in_specs=[pl.BlockSpec(memory_space=pltpu.SMEM)] + [pl.BlockSpec(memory_space=pl.ANY)] * 4,
        out_specs=[pl.BlockSpec(memory_space=pl.ANY)] * 3,
        scratch_shapes=[
            pltpu.VMEM((3, rows, width), jnp.bfloat16),
            pltpu.SemaphoreType.DMA((3, 4)),
            pltpu.SemaphoreType.DMA((3,)),
        ],
        cost_estimate=pl.CostEstimate(flops=0, bytes_accessed=12 * rows * width, transcendentals=0),
        name="pack",
    )(links, *arrays)


def dot_nt(a, b):
    return lax.dot_general(a, b, (((1,), (1,)), ((), ())), preferred_element_type=jnp.float32)


def dot_nn(a, b):
    return lax.dot_general(a, b, (((1,), (0,)), ((), ())), preferred_element_type=jnp.float32)


def dot_tn(a, b):
    return lax.dot_general(a, b, (((0,), (0,)), ((), ())), preferred_element_type=jnp.float32)


def attend_kernel(first_head, heads, heads_dev, score_scale, num_previous, sink, links, sink_in, *refs):
    arrays, ins, flag_ins, refs = refs[:4], refs[4:7], refs[7:10], refs[10 + num_previous :]
    outs, own_outs, sink_out = refs[:3], refs[3:6], refs[6]
    held, flags_held, grads, own_sems, in_sems, flag_sems, own_out_sems, out_sems = refs[7:]
    me = lax.axis_index("dp")
    blocks = 4

    def own_columns(head):
        return pl.ds(pl.multiple_of((me * heads_dev + first_head + head) * BLOCK, BLOCK), BLOCK)

    def columns(head):
        return pl.ds(head * BLOCK, BLOCK)

    loads = [
        [
            pltpu.make_async_copy(
                array.at[0, :, own_columns(head)],
                held.at[me, pl.ds(num * BLOCK, BLOCK), columns(head)],
                own_sems.at[head, num],
            )
            for num, array in enumerate(arrays)
        ]
        + [
            pltpu.make_async_copy(
                ins[place].at[pl.ds(0, 4 * BLOCK), columns(head)],
                held.at[me ^ mask, :, columns(head)],
                in_sems.at[head, place],
            )
            for place, mask in enumerate(ORDER)
        ]
        for head in range(heads)
    ]
    for group in loads:
        for copy in group:
            copy.start()
    flag_loads = [
        pltpu.make_async_copy(
            flag_ins[place].at[pl.ds(4 * BLOCK, FLAG_ROWS), pl.ds(0, BLOCK)],
            flags_held.at[me ^ mask],
            flag_sems.at[place],
        )
        for place, mask in enumerate(ORDER)
    ]
    for copy in flag_loads:
        copy.start()
    flags_held[me] = live_flags(links, BLOCK)
    keys_iota = lax.broadcasted_iota(jnp.int32, (BLOCK, BLOCK), 0)
    queries_iota = lax.broadcasted_iota(jnp.int32, (BLOCK, BLOCK), 1)
    causal = keys_iota <= queries_iota
    lanes = lax.broadcasted_iota(jnp.int32, (8, BLOCK), 1)
    sink_sum = sink_in[...]
    for copy in flag_loads:
        copy.wait()
    stores = []
    for head in range(heads):
        for copy in loads[head]:
            copy.wait()
        cols = columns(head)

        def part(kind, first, last):
            return held[first : last + 1, kind * BLOCK : (kind + 1) * BLOCK, cols].reshape(
                (last + 1 - first) * BLOCK, BLOCK
            )

        sink_logit = sink[me * heads_dev + first_head + head] * LOG2_E
        scores, prob_grads = {}, {}
        for pair in range(0, blocks, 2):
            first = max(0, pair - LEVELS)
            score = dot_nt(part(1, first, pair + 1), part(0, pair, pair + 1))
            prob_grad = dot_nt(part(2, first, pair + 1), part(3, pair, pair + 1))
            for block in (pair, pair + 1):
                lanes_here = slice((block - pair) * BLOCK, (block - pair + 1) * BLOCK)
                for source in range(max(0, block - LEVELS), block + 1):
                    rows = slice((source - first) * BLOCK, (source - first + 1) * BLOCK)
                    scores[block, source] = score[rows, lanes_here]
                    prob_grads[block, source] = prob_grad[rows, lanes_here]
        sink_total = jnp.zeros((1, BLOCK), jnp.float32)
        weights, score_grads = {}, {}
        for block in range(blocks):
            sources = range(max(0, block - LEVELS), block + 1)
            flags = flags_held[block].astype(jnp.float32)
            pieces = []
            for source in sources:
                piece = scores[block, source] * (score_scale * LOG2_E)
                if source == block:
                    piece = jnp.where(causal, piece, NEG_FILL)
                else:
                    row = 8 * (block - source - 1)
                    piece = jnp.where(flags[row : row + 1] > 0.5, piece, NEG_FILL)
                pieces.append(piece)
            row_max = functools.reduce(jnp.maximum, pieces)
            row_max = jnp.maximum(jnp.max(row_max, axis=0, keepdims=True), sink_logit)
            pieces = [jnp.exp2(piece - row_max) for piece in pieces]
            sink_exp = jnp.exp2(sink_logit - row_max)
            denominator = jnp.sum(functools.reduce(jnp.add, pieces), axis=0, keepdims=True) + sink_exp
            scale = 1.0 / denominator
            pieces = [piece * scale for piece in pieces]
            products = [piece * prob_grads[block, source] for piece, source in zip(pieces, sources)]
            row_delta = jnp.sum(functools.reduce(jnp.add, products), axis=0, keepdims=True)
            sink_total = sink_total + sink_exp * scale * row_delta
            for piece, source in zip(pieces, sources):
                weights[block, source] = piece.astype(jnp.bfloat16)
                score_grads[block, source] = (
                    piece * (prob_grads[block, source] - row_delta)
                ).astype(jnp.bfloat16)
        here = lanes == me * heads_dev + first_head + head
        sink_sum = sink_sum - jnp.where(here, jnp.sum(sink_total, axis=1, keepdims=True), 0.0)
        for block in range(blocks):
            first = max(0, block - LEVELS)
            score_grad = jnp.concatenate([score_grads[block, b] for b in range(first, block + 1)], axis=0)
            query_grad = dot_tn(score_grad, part(1, first, block)) * score_scale
            grads[block, 0:BLOCK, cols] = query_grad.astype(jnp.bfloat16)
        for source in range(blocks):
            last = min(blocks - 1, source + LEVELS)
            score_grad = jnp.concatenate([score_grads[b, source] for b in range(source, last + 1)], axis=1)
            weight = jnp.concatenate([weights[b, source] for b in range(source, last + 1)], axis=1)
            key_grad = dot_nn(score_grad, part(0, source, last)) * score_scale
            value_grad = dot_nn(weight, part(3, source, last))
            grads[source, BLOCK : 2 * BLOCK, cols] = key_grad.astype(jnp.bfloat16)
            grads[source, 2 * BLOCK : 3 * BLOCK, cols] = value_grad.astype(jnp.bfloat16)
        copies = [
            pltpu.make_async_copy(
                grads.at[me ^ mask, :, cols], outs[place].at[:, cols], out_sems.at[head, place]
            )
            for place, mask in enumerate(ORDER)
        ] + [
            pltpu.make_async_copy(
                grads.at[me, pl.ds(num * BLOCK, BLOCK), cols],
                out.at[0, :, own_columns(head)],
                own_out_sems.at[head, num],
            )
            for num, out in enumerate(own_outs)
        ]
        for copy in copies:
            copy.start()
        stores.extend(copies)
    sink_out[...] = sink_sum
    for copy in stores:
        copy.wait()


def attend(sink_logit, links, sink_sum, arrays, packed, flags, previous, first_head, heads, heads_dev, score_scale):
    rows, grad_rows, width = 4 * BLOCK, 3 * BLOCK, packed[0].shape[1]
    hbm = pl.BlockSpec(memory_space=pl.ANY)
    smem = pl.BlockSpec(memory_space=pltpu.SMEM)
    vmem = pl.BlockSpec(memory_space=pltpu.VMEM)
    return pl.pallas_call(
        functools.partial(attend_kernel, first_head, heads, heads_dev, score_scale, len(previous)),
        out_shape=[jax.ShapeDtypeStruct((grad_rows, width), jnp.bfloat16)] * 3
        + [jax.ShapeDtypeStruct(arrays[0].shape, jnp.bfloat16)] * 3
        + [jax.ShapeDtypeStruct((8, BLOCK), jnp.float32)],
        in_specs=[smem, smem, vmem] + [hbm] * (10 + len(previous)),
        out_specs=[hbm] * 6 + [vmem],
        scratch_shapes=[
            pltpu.VMEM((4, rows, width), jnp.bfloat16),
            pltpu.VMEM((4, FLAG_ROWS, BLOCK), jnp.bfloat16),
            pltpu.VMEM((4, grad_rows, width), jnp.bfloat16),
            pltpu.SemaphoreType.DMA((heads, 4)),
            pltpu.SemaphoreType.DMA((heads, 3)),
            pltpu.SemaphoreType.DMA((3,)),
            pltpu.SemaphoreType.DMA((heads, 3)),
            pltpu.SemaphoreType.DMA((heads, 3)),
        ],
        input_output_aliases={13 + num: 3 + num for num in range(len(previous))},
        compiler_params=pltpu.CompilerParams(vmem_limit_bytes=8 * 2**20),
        cost_estimate=pl.CostEstimate(flops=0, bytes_accessed=0, transcendentals=0),
        name="attend",
    )(sink_logit, links, sink_sum, *arrays, *packed, *flags, *previous)


def unpack_kernel(offset, width, share, *refs):
    ins, outs, (held, load_sems, store_sems) = refs[:3], refs[6:9], refs[9:]
    me = lax.axis_index("dp")
    loads = [
        pltpu.make_async_copy(ins[place], held.at[place], load_sems.at[place]) for place in range(3)
    ]
    for copy in loads:
        copy.start()
    stores = []
    for place, mask in enumerate(ORDER):
        loads[place].wait()
        start = pl.multiple_of((me ^ mask) * share + offset, BLOCK)
        for num, out in enumerate(outs):
            stores.append(
                pltpu.make_async_copy(
                    held.at[place, pl.ds(num * BLOCK, BLOCK), :],
                    out.at[0, :, pl.ds(start, width)],
                    store_sems.at[place, num],
                )
            )
            stores[-1].start()
    for copy in stores:
        copy.wait()


def unpack(parts, previous, offset, share):
    rows, width = parts[0].shape
    return pl.pallas_call(
        functools.partial(unpack_kernel, offset, width, share),
        out_shape=[jax.ShapeDtypeStruct(out.shape, out.dtype) for out in previous],
        in_specs=[pl.BlockSpec(memory_space=pl.ANY)] * 6,
        out_specs=[pl.BlockSpec(memory_space=pl.ANY)] * 3,
        scratch_shapes=[
            pltpu.VMEM((3, rows, width), jnp.bfloat16),
            pltpu.SemaphoreType.DMA((3,)),
            pltpu.SemaphoreType.DMA((3, 3)),
        ],
        input_output_aliases={3 + num: num for num in range(3)},
        compiler_params=pltpu.CompilerParams(vmem_limit_bytes=8 * 2**20),
        cost_estimate=pl.CostEstimate(flops=0, bytes_accessed=0, transcendentals=0),
        name="unpack",
    )(*parts, *previous)


def swap(value, axis, mask):
    return lax.ppermute(value, axis, [(i, i ^ mask) for i in range(lax.axis_size(axis))])


def after(value, other):
    return lax.optimization_barrier((value, other))


def add_swapped(value, axis, masks):
    for mask in masks:
        value = value + swap(value, axis, mask)
    return value


def head_shares_body(chunks, queries, key_states, values, out_grad, block_links, sink_logit):
    heads = sink_logit.shape[0]
    head_size = queries.shape[2] // heads
    score_scale = head_size ** (-0.5)
    heads_dev = heads // 4
    share = heads_dev * head_size
    arrays = (queries, key_states, values, out_grad)
    links = block_links.reshape(LEVELS)
    received, first = [], 0
    for count in chunks:
        packed = pack(links, arrays, first * head_size, count * head_size, share, first == 0)
        moved = [swap(part, "dp", mask) for part, mask in zip(packed, ORDER)]
        received.append((first, count, moved))
        first += count
    results, outputs, sink_sum = [], [], jnp.zeros((8, BLOCK), jnp.float32)
    for num, (first, count, packed) in enumerate(received):
        *grads, sink_sum = attend(
            sink_logit, links, sink_sum, arrays, packed, received[0][2], outputs, first, count, heads_dev, score_scale
        )
        grads, outputs = grads[:3], list(grads[3:])
        if num:
            sink_sum = sink_sum + swap(sink_sum, "ctx", 2)
            grads[0], results[0][1][0] = after(grads[0], results[0][1][0])
        else:
            for place in range(3):
                grads[place], received[1][2][0] = after(grads[place], received[1][2][0])
        results.append((first, [swap(grad, "dp", mask) for grad, mask in zip(grads, ORDER)]))
    sink_sum, results[0][1][2] = after(sink_sum, results[0][1][2])
    once = jnp.minimum(links[0] + 2, 1)
    sink_sum = lax.fori_loop(0, once, lambda _, held: add_swapped(held, "ctx", (1, 4)), sink_sum)
    sink_sum = add_swapped(sink_sum, "dp", (1,))
    outputs = list(unpack(results[0][1], outputs, results[0][0] * head_size, share))
    sink_sum, outputs[0] = after(sink_sum, outputs[0])
    sink_sum = add_swapped(sink_sum, "dp", (2,))
    outputs = unpack(results[1][1], outputs, results[1][0] * head_size, share)
    return (*outputs, sink_sum[0, :heads])


def from_behind(value, axis, steps):
    count = lax.axis_size(axis)
    initial, last = (max(0, -steps), min(count, count - steps))
    return lax.ppermute(value, axis, [(source, source + steps) for source in range(initial, last)])


def causal_table(block_len):
    rows_iota = lax.broadcasted_iota(jnp.int32, (block_len, block_len), 0)
    cols_iota = lax.broadcasted_iota(jnp.int32, (block_len, block_len), 1)
    return rows_iota >= cols_iota


def attend_forward(q_blocks, key_all, val_all, allowed, sink_logit, score_scale):
    scores = (
        jnp.einsum("bqhd,bkhd->bhqk", q_blocks, key_all, preferred_element_type=jnp.float32)
        * score_scale
    )
    scores = jnp.where(allowed[:, None], scores, NEG_FILL)
    row_max = jnp.maximum(jnp.max(scores, axis=-1), sink_logit[None, :, None])
    exp_scores = jnp.exp(scores - row_max[..., None])
    sink_exp = jnp.exp(sink_logit[None, :, None] - row_max)
    denominator = jnp.sum(exp_scores, axis=-1) + sink_exp
    soft_prob = exp_scores / denominator[..., None]
    sink_prob = sink_exp / denominator
    weights = soft_prob.astype(jnp.bfloat16)
    output = jnp.einsum(
        "bhqk,bkhd->bqhd", weights, val_all, preferred_element_type=jnp.float32
    ).astype(jnp.bfloat16)
    return (soft_prob, weights, sink_prob, output)


def attend_backward(
    q_blocks, key_all, val_all, grad_blocks, soft_prob, weights, sink_prob, output, score_scale
):
    row_delta = jnp.sum(grad_blocks.astype(jnp.float32) * output.astype(jnp.float32), axis=-1)
    row_delta = jnp.transpose(row_delta, (0, 2, 1))
    prob_grad = jnp.einsum(
        "bqhd,bkhd->bhqk", grad_blocks, val_all, preferred_element_type=jnp.float32
    )
    score_grad = (soft_prob * (prob_grad - row_delta[..., None])).astype(jnp.bfloat16)
    query_grad = (
        jnp.einsum("bhqk,bkhd->bqhd", score_grad, key_all, preferred_element_type=jnp.float32)
        * score_scale
    ).astype(jnp.bfloat16)
    key_terms = (
        jnp.einsum("bhqk,bqhd->bkhd", score_grad, q_blocks, preferred_element_type=jnp.float32)
        * score_scale
    )
    value_terms = jnp.einsum(
        "bhqk,bqhd->bkhd", weights, grad_blocks, preferred_element_type=jnp.float32
    )
    sink_term = -jnp.sum(sink_prob * row_delta, axis=(0, 2))
    return (query_grad, key_terms, value_terms, sink_term)


def keys_travel_body(queries, key_states, values, out_grad, block_links, sink_logit):
    tokens = queries.shape[1]
    width = queries.shape[2]
    blocks = tokens // BLOCK
    heads = sink_logit.shape[0]
    head_size = width // heads
    score_scale = head_size ** (-0.5)

    def to_blocks(array):
        return array.reshape(blocks, BLOCK, heads, head_size)

    q_blocks = to_blocks(queries)
    grad_blocks = to_blocks(out_grad)
    level_live = block_links >= 0
    causal = jnp.broadcast_to(causal_table(BLOCK), (blocks, BLOCK, BLOCK))
    remote_masks = [
        jnp.broadcast_to(level_live[level_num][:, None, None], (blocks, BLOCK, BLOCK))
        for level_num in range(LEVELS)
    ]
    allowed = jnp.concatenate([causal] + remote_masks, axis=2)
    fetched = []
    for level_num in range(LEVELS):
        fetched.append(from_behind((key_states, values), "dp", 2**level_num))
    key_all = jnp.concatenate(
        [to_blocks(key_states)] + [to_blocks(moved[0]) for moved in fetched], axis=1
    )
    val_all = jnp.concatenate(
        [to_blocks(values)] + [to_blocks(moved[1]) for moved in fetched], axis=1
    )
    soft_prob, weights, sink_prob, output = attend_forward(
        q_blocks, key_all, val_all, allowed, sink_logit, score_scale
    )
    query_grad, key_terms, value_terms, sink_term = attend_backward(
        q_blocks, key_all, val_all, grad_blocks, soft_prob, weights, sink_prob, output, score_scale
    )
    key_grad = key_terms[:, :BLOCK].reshape(1, tokens, width)
    value_grad = value_terms[:, :BLOCK].reshape(1, tokens, width)
    for level_num in range(LEVELS):
        first_col = BLOCK * (1 + level_num)
        key_part = (
            key_terms[:, first_col : first_col + BLOCK]
            .reshape(1, tokens, width)
            .astype(jnp.bfloat16)
        )
        value_part = (
            value_terms[:, first_col : first_col + BLOCK]
            .reshape(1, tokens, width)
            .astype(jnp.bfloat16)
        )
        key_back, value_back = from_behind((key_part, value_part), "dp", -(2**level_num))
        key_grad = key_grad + key_back.astype(jnp.float32)
        value_grad = value_grad + value_back.astype(jnp.float32)
    sink_grad = lax.psum(sink_term, ("dp", "ctx"))
    return (
        query_grad.reshape(1, tokens, width),
        key_grad.astype(jnp.bfloat16),
        value_grad.astype(jnp.bfloat16),
        sink_grad,
    )


CHUNKS = (2, 3)


def body(queries, key_states, values, out_grad, block_links, sink_logit):
    heads = sink_logit.shape[0]
    blocks = lax.axis_size("dp")
    groups = lax.axis_size("ctx")
    fits = (
        blocks == 4
        and queries.shape[:2] == (1, BLOCK)
        and queries.shape[2] == heads * BLOCK
        and heads == 4 * sum(CHUNKS)
        and groups == 8
    )
    plan = functools.partial(head_shares_body, CHUNKS) if fits else keys_travel_body
    return plan(queries, key_states, values, out_grad, block_links, sink_logit)


def solution(mesh):
    placed = (
        P("ctx", "dp", None),
        P("ctx", "dp", None),
        P("ctx", "dp", None),
        P("ctx", "dp", None),
        P(None, "dp"),
        P(),
    )
    return jax.shard_map(
        body,
        mesh=mesh,
        in_specs=placed,
        out_specs=(P("ctx", "dp", None), P("ctx", "dp", None), P("ctx", "dp", None), P()),
        check_vma=False,
    )
```
